32 devices in a mesh: pipe: 8 (over z, x), expert: 4 (over y, core).
Axes of the slice: x: 2, y: 2, z: 4, core: 2. Of those that a mesh axis runs over, the one named last changes fastest.
Arguments:
- upstream: bfloat16 [8, 1024, 7168], P('pipe', None, 'expert'), may hold values from -6 to 6
- shared_down: bfloat16 [8, 1024, 7168], P('pipe', None, 'expert'), may hold values from -0.0625 to 0.0625
- shared_gate: bfloat16 [8, 7168, 1024], P('pipe', 'expert'), may hold values from -0.1875 to 0.1875
- shared_up: bfloat16 [8, 7168, 1024], P('pipe', 'expert'), may hold values from -0.1875 to 0.1875
- router_weight: bfloat16 [8, 7168, 256], P('pipe', 'expert'), may hold values from -2 to 2
- gate_pre: bfloat16 [8, 1024, 1024], P('pipe', 'expert'), may hold values from -6 to 6
- up_pre: bfloat16 [8, 1024, 1024], P('pipe', 'expert'), may hold values from -6 to 6
- gate_grad: float32 [8, 1024, 8], P('pipe'), may hold values from -6 to 6
- gate_scores: float32 [8, 1024, 8], P('pipe'), may hold values from 0.05 to 0.95
- expert_ids: int32 [8, 1024, 8], P('pipe'), may hold values from 0 to 255, all different within a row
Outputs:
- down_grad: bfloat16 [8, 1024, 7168], P('pipe', None, 'expert')
The draws below stay inside these ranges and needn't reach their ends.
Inputs may be any that keep to these rules, and one draw needn't show every extreme that they name: `expert_ids`: each token names 8 different experts.
All inputs are finite; a program needn't handle non-finite values.
Results may differ from the reference program's by a relative error of at most 0.02.
Values may be sent and summed in bfloat16 or wider, within the bound.
No kernel may reach another device: no remote copies, remote signals or barrier semaphores. Data moves between devices by JAX's collectives and lax.ppermute only.
A program may use at most 64 MiB of HBM per device.

```python
import jax
import jax.numpy as jnp
from jax import lax

D = 7168
NEXP = 256
TOP = 8
HID = 1024
TOK = 1024
N_PIPE = 8
N_EXPERT = 4


def steps_of(own_key, dims, shards, low, high):
    def one(dim, parts):
        steps = jax.random.uniform(jax.random.fold_in(jax.random.fold_in(own_key, 6), dim), (parts,), jnp.float32, low / len(shards), high / len(shards))
        return jnp.repeat(jnp.exp(steps), dims[dim] // parts).reshape((-1,) + (1,) * (len(dims) - dim - 1))

    level = one(*shards[0])
    for cut in shards[1:]:
        level = level * one(*cut)
    return level


def different_ones(rng, rows, amount, top, lift):
    ranking = jax.random.permutation(jax.random.fold_in(rng, 1), amount)
    boost = ranking
    for power in range(3):
        boost = boost * boost // amount
    boost = boost * lift // amount
    chance = jax.random.randint(jax.random.fold_in(rng, 2), (rows, amount), 0, 4096) + boost
    holders = jax.random.permutation(jax.random.fold_in(rng, 3), rows)[jnp.arange(amount) % rows]
    chance = jnp.where(jnp.arange(rows)[:, None] == holders[None, :], 1 << 14, chance)
    score = chance * amount + jnp.arange(amount)
    return lax.top_k(score.astype(jnp.int32), top)[1].astype(jnp.int32)


def noise(key, dims, scale, most, shards=(), kind=jnp.bfloat16):
    loudness = steps_of(key, dims, shards, -0.22, 0.18) if shards else 1.0
    values = jax.random.normal(key, dims, jnp.float32) * scale * loudness
    return jnp.minimum(jnp.maximum(values, -most), most).astype(kind)


def setup_inputs(seed: int = 0) -> dict:
    keys = jax.random.split(jax.random.key(seed), 11)
    return {
        "upstream": noise(keys[0], (N_PIPE, TOK, D), 1.0, 6.0, ((0, 8), (2, 4))),
        "shared_down": noise(keys[1], (N_PIPE, HID, D), D ** -0.5, 0.0625, ((0, 8), (2, 4))),
        "shared_gate": noise(keys[2], (N_PIPE, D, HID), HID ** -0.5, 0.1875, ((0, 8), (1, 4))),
        "shared_up": noise(keys[3], (N_PIPE, D, HID), HID ** -0.5, 0.1875, ((0, 8), (1, 4))),
        "router_weight": noise(keys[4], (N_PIPE, D, NEXP), TOP ** -0.5, 2.0, ((0, 8), (1, 4))),
        "gate_pre": noise(keys[5], (N_PIPE, TOK, HID), 1.0, 6.0, ((0, 8), (1, 4))),
        "up_pre": noise(keys[6], (N_PIPE, TOK, HID), 1.0, 6.0, ((0, 8), (1, 4))),
        "gate_grad": noise(keys[7], (N_PIPE, TOK, TOP), 1.0, 6.0, ((0, 8),), jnp.float32),
        "gate_scores": jnp.clip(0.05 + 0.9 * jax.random.uniform(keys[8], (N_PIPE, TOK, TOP), jnp.float32) ** steps_of(keys[8], (N_PIPE, TOK, TOP), ((0, 8),), -0.2, 0.2), 0.05, 0.95),
        "expert_ids": different_ones(keys[9], N_PIPE * TOK, NEXP, TOP, 512).reshape((N_PIPE, TOK, TOP)),
    }


def section_backward(params):
    incoming, w_down, w_gate, w_up, w_router, pre_gate, pre_up, grad_gate, scores, chosen = params
    width = incoming.shape[1] // N_EXPERT
    hidden_grad = jnp.zeros((incoming.shape[0], w_down.shape[0]), jnp.float32)
    for block in range(N_EXPERT):
        part = jnp.dot(incoming[:, block * width:(block + 1) * width], w_down[:, block * width:(block + 1) * width].T, preferred_element_type=jnp.float32)
        hidden_grad = hidden_grad + part.astype(jnp.bfloat16).astype(jnp.float32)
    act_a = pre_gate.astype(jnp.float32)
    act_b = pre_up.astype(jnp.float32)
    sigma = jax.nn.sigmoid(act_a)
    gate_part = (hidden_grad * act_b * sigma * (1.0 + act_a * (1.0 - sigma))).astype(jnp.bfloat16)
    up_part = (hidden_grad * act_a * sigma).astype(jnp.bfloat16)
    total = jnp.sum(scores, axis=-1, keepdims=True)
    mixed = jnp.sum(grad_gate * scores, axis=-1, keepdims=True)
    logit_grad = 2.5 * (grad_gate - mixed / total) / total * scores * (1.0 - scores)
    columns = jnp.arange(NEXP, dtype=jnp.int32)
    dense = jnp.zeros((grad_gate.shape[0], NEXP), jnp.float32)
    for slot in range(TOP):
        dense = dense + jnp.where(chosen[:, slot:slot + 1] == columns[None, :], logit_grad[:, slot:slot + 1], 0.0)
    dense_grad = dense.astype(jnp.bfloat16)
    result = jnp.dot(gate_part, w_gate.T, preferred_element_type=jnp.float32)
    result = result + jnp.dot(up_part, w_up.T, preferred_element_type=jnp.float32)
    result = result + jnp.dot(dense_grad, w_router.T, preferred_element_type=jnp.float32)
    return result.astype(jnp.bfloat16)


def reference(upstream, shared_down, shared_gate, shared_up, router_weight, gate_pre, up_pre, gate_grad, gate_scores, expert_ids):
    def ahead(arr, steps):
        return jnp.roll(arr, -steps, axis=0)
    params = (ahead(upstream, 2), ahead(shared_down, 1), ahead(shared_gate, 1), ahead(shared_up, 1),
              ahead(router_weight, 1), ahead(gate_pre, 1), ahead(up_pre, 1), ahead(gate_grad, 1),
              ahead(gate_scores, 1), ahead(expert_ids, 1))
    return lax.map(section_backward, params)
```

```python
import jax
import jax.numpy as jnp
from jax import lax
from jax.sharding import PartitionSpec as P

CHUNKS = 4
IN_FLIGHT = 2


def back_one(x):
    length = lax.axis_size("pipe")
    return lax.ppermute(x, "pipe", [(i, (i - 1) % length) for i in range(length)])


def contract_last(left, right):
    return lax.dot_general(
        left, right, (((1,), (1,)), ((), ())), preferred_element_type=jnp.float32
    )


def sum_to_owners(blocks):
    n = lax.axis_size("expert")
    me = lax.axis_index("expert")
    total = lax.dynamic_index_in_dim(blocks, me, keepdims=False).astype(jnp.float32)
    for step in range(1, n):
        part = lax.dynamic_index_in_dim(blocks, (me + step) % n, keepdims=False)
        part = lax.ppermute(part, "expert", [(i, (i + step) % n) for i in range(n)])
        total = total + part.astype(jnp.float32)
    return total


def gather_chips(own):
    n = lax.axis_size("expert")
    chips, chip = n // 2, lax.axis_index("expert") // 2
    held = lax.dynamic_update_index_in_dim(
        jnp.zeros((chips,) + own.shape, own.dtype), own, chip, 0
    )
    for step in range(1, chips):
        part = lax.ppermute(own, "expert", [(i, (i + 2 * step) % n) for i in range(n)])
        held = lax.dynamic_update_index_in_dim(held, part, (chip - step) % chips, 0)
    return held


def gather_cores(held):
    n = lax.axis_size("expert")
    core = lax.axis_index("expert") % 2
    other = lax.ppermute(held, "expert", [(i, i ^ 1) for i in range(n)])
    first = jnp.where(core == 0, held, other)
    second = jnp.where(core == 0, other, held)
    return jnp.stack([first, second], axis=1).reshape(n, *held.shape[1:])


def in_order(later, earlier):
    return lax.optimization_barrier((later, earlier))


def routed_grad(grad_gate, scores, chosen, n_experts):
    total = jnp.sum(scores, axis=-1, keepdims=True)
    mixed = jnp.sum(grad_gate * scores, axis=-1, keepdims=True)
    logit_grad = 2.5 * (grad_gate - mixed / total) / total * scores * (1.0 - scores)
    columns = lax.broadcasted_iota(jnp.int32, (1, n_experts), 1)
    dense = jnp.zeros((grad_gate.shape[0], n_experts), jnp.float32)
    for slot in range(grad_gate.shape[1]):
        dense = dense + jnp.where(
            chosen[:, slot : slot + 1] == columns, logit_grad[:, slot : slot + 1], 0.0
        )
    return dense.astype(jnp.bfloat16)


def shards(
    upstream,
    shared_down,
    shared_gate,
    shared_up,
    router_weight,
    gate_pre,
    up_pre,
    gate_grad,
    gate_scores,
    expert_ids,
):
    n = lax.axis_size("expert")
    tokens, width = upstream.shape[1:]
    hidden = shared_down.shape[1]
    rows = tokens // n
    chunks = min(CHUNKS, rows // 16)
    part = rows // chunks
    w_down, w_gate, w_up, w_router = (
        shared_down[0],
        shared_gate[0],
        shared_up[0],
        router_weight[0],
    )
    dense = routed_grad(gate_grad[0], gate_scores[0], expert_ids[0], w_router.shape[1])
    dense = dense.reshape(n, rows, -1)
    grads = upstream.reshape(n, rows, width)
    arrived = []
    for c in range(chunks):
        piece = grads[:, c * part : (c + 1) * part].reshape(n * part, width)
        if c >= IN_FLIGHT:
            piece, arrived[c - IN_FLIGHT] = in_order(piece, arrived[c - IN_FLIGHT])
        arrived.append(back_one(piece))

    def first_product(c):
        partial = contract_last(arrived[c], w_down).astype(jnp.bfloat16)
        return partial.reshape(n, part, hidden)

    def activation(c, hidden_grad):
        here = slice(c * part, (c + 1) * part)
        act_a = gate_pre[0, here].astype(jnp.float32)
        act_b = up_pre[0, here].astype(jnp.float32)
        sigma = jax.nn.sigmoid(act_a)
        gate_part = hidden_grad * act_b * sigma * (1.0 + act_a * (1.0 - sigma))
        up_part = hidden_grad * act_a * sigma
        return jnp.concatenate([gate_part, up_part], axis=1).astype(jnp.bfloat16)

    def second_product(c, both):
        both = both.reshape(n * part, 2 * hidden)
        routed = dense[:, c * part : (c + 1) * part].reshape(n * part, -1)
        result = contract_last(both[:, :hidden], w_gate)
        result = result + contract_last(both[:, hidden:], w_up)
        result = result + contract_last(routed, w_router)
        return result.astype(jnp.bfloat16)

    out = jnp.zeros((n, rows, width), jnp.bfloat16)
    own = activation(0, sum_to_owners(first_product(0)))
    for c in range(chunks):
        by_chip = gather_chips(own)
        if c + 1 < chunks:
            arrived[c + 1], own = in_order(arrived[c + 1], own)
            partial = first_product(c + 1)
            partial, by_chip = in_order(partial, by_chip)
            hidden_grad = sum_to_owners(partial)
        result = second_product(c, gather_cores(by_chip))
        if c + 1 < chunks:
            hidden_grad, result = in_order(hidden_grad, result)
            own = activation(c + 1, hidden_grad)
        result = back_one(result).reshape(n, part, width)
        out = lax.dynamic_update_slice(out, result, (0, c * part, 0))
    return out.reshape(1, tokens, width)


def solution(mesh):
    in_specs = (
        P("pipe", None, "expert"),
        P("pipe", None, "expert"),
        P("pipe", "expert", None),
        P("pipe", "expert", None),
        P("pipe", "expert", None),
        P("pipe", "expert", None),
        P("pipe", "expert", None),
        P("pipe", None, None),
        P("pipe", None, None),
        P("pipe", None, None),
    )
    out_specs = P("pipe", None, "expert")
    return jax.shard_map(shards, mesh=mesh, in_specs=in_specs, out_specs=out_specs, check_vma=False)
```

```python
import functools

import jax
import jax.numpy as jnp
from jax import lax
from jax.experimental import pallas as pl
from jax.experimental.pallas import tpu as pltpu
from jax.sharding import PartitionSpec as P

CHUNKS = 4
FREE = pl.CostEstimate(flops=0, bytes_accessed=0, transcendentals=0)
FAR = pl.BlockSpec(memory_space=pl.ANY)


def params(**kwargs):
    return pltpu.CompilerParams(vmem_limit_bytes=24 * 1024 * 1024, **kwargs)


def block_of(size, most):
    fits = [b for b in range(128, min(size, most) + 1, 128) if size % b == 0]
    return fits[-1] if fits else size


def back_one(x):
    length = lax.axis_size("pipe")
    return lax.ppermute(x, "pipe", [(i, (i - 1) % length) for i in range(length)])


def to_expert(x, by):
    n = lax.axis_size("expert")
    return lax.ppermute(x, "expert", [(i, (i + by) % n) for i in range(n)])


def to_other_core(x):
    n = lax.axis_size("expert")
    return lax.ppermute(x, "expert", [(i, i ^ 1) for i in range(n)])


def in_order(later, earlier):
    return lax.optimization_barrier((later, earlier))


def contract_last(left, right):
    return lax.dot_general(
        left, right, (((1,), (1,)), ((), ())), preferred_element_type=jnp.float32
    )


def take_kernel(source_ref, out_ref):
    out_ref[...] = source_ref[...]


def put_kernel(source_ref, *refs):
    refs[-1][...] = source_ref[...]


def take_rows(array, c, part):
    n, _, width = array.shape
    return pl.pallas_call(
        take_kernel,
        out_shape=jax.ShapeDtypeStruct((n, part, width), array.dtype),
        grid=(n,),
        in_specs=[pl.BlockSpec((1, part, width), lambda i: (i, c, 0))],
        out_specs=pl.BlockSpec((1, part, width), lambda i: (i, 0, 0)),
        cost_estimate=FREE,
        name="take_rows",
    )(array)


def put_rows(out, piece, c, rows):
    n, part, width = piece.shape
    spec = pl.BlockSpec((1, part, width), lambda i: (i, 0, 0))
    return pl.pallas_call(
        put_kernel,
        out_shape=jax.ShapeDtypeStruct((n, rows, width), piece.dtype),
        grid=(n,),
        in_specs=[spec] + ([] if out is None else [FAR]),
        out_specs=pl.BlockSpec((1, part, width), lambda i: (i, c, 0)),
        input_output_aliases={} if out is None else {1: 0},
        cost_estimate=FREE,
        name="put_rows",
    )(*((piece,) if out is None else (piece, out)))


def routed_kernel(grad_ref, score_ref, chosen_ref, out_ref):
    grad, scores, chosen = grad_ref[...], score_ref[...], chosen_ref[...]
    total = jnp.sum(scores, axis=-1, keepdims=True)
    mixed = jnp.sum(grad * scores, axis=-1, keepdims=True)
    logit_grad = 2.5 * (grad - mixed / total) / total * scores * (1.0 - scores)
    columns = lax.broadcasted_iota(jnp.int32, out_ref.shape, 1)
    dense = jnp.zeros(out_ref.shape, jnp.float32)
    for slot in range(grad.shape[1]):
        here = chosen[:, slot : slot + 1] == columns
        dense = dense + jnp.where(here, logit_grad[:, slot : slot + 1], 0.0)
    out_ref[...] = dense.astype(out_ref.dtype)


def routed_grad(grad, scores, chosen, n_experts):
    tokens, top = grad.shape
    block = min(tokens, 128)
    spec = pl.BlockSpec((block, top), lambda i: (i, 0))
    return pl.pallas_call(
        routed_kernel,
        out_shape=jax.ShapeDtypeStruct((tokens, n_experts), jnp.bfloat16),
        grid=(tokens // block,),
        in_specs=[spec, spec, spec],
        out_specs=pl.BlockSpec((block, n_experts), lambda i: (i, 0)),
        cost_estimate=FREE,
        name="routed_grad",
    )(grad, scores, chosen)


def first_kernel(n, me_ref, rows_ref, weight_ref, *out_refs):
    me = me_ref[0]
    part = rows_ref.shape[1]
    left = jnp.concatenate([rows_ref[lax.rem(me + j, n)] for j in range(n)], axis=0)
    product = contract_last(left, weight_ref[...]).astype(jnp.bfloat16)
    for j in range(n):
        out_refs[j][...] = product[j * part : (j + 1) * part]


def first_product(me, rows, weight):
    n, part, width = rows.shape
    hidden = weight.shape[0]
    block = block_of(hidden, 256)
    return pl.pallas_call(
        functools.partial(first_kernel, n),
        out_shape=[jax.ShapeDtypeStruct((part, hidden), jnp.bfloat16)] * n,
        grid_spec=pltpu.PrefetchScalarGridSpec(
            num_scalar_prefetch=1,
            grid=(hidden // block,),
            in_specs=[
                pl.BlockSpec((n, part, width), lambda i, me: (0, 0, 0)),
                pl.BlockSpec((block, width), lambda i, me: (i, 0)),
            ],
            out_specs=[pl.BlockSpec((part, block), lambda i, me: (0, i))] * n,
        ),
        compiler_params=params(),
        cost_estimate=FREE,
        name="first_product",
    )(me, rows, weight)


def activation_kernel(gate_ref, up_ref, *refs):
    *part_refs, out_ref = refs
    hidden = gate_ref.shape[1]
    hidden_grad = part_refs[0][...].astype(jnp.float32)
    for ref in part_refs[1:]:
        hidden_grad = hidden_grad + ref[...].astype(jnp.float32)
    act_a = gate_ref[...].astype(jnp.float32)
    act_b = up_ref[...].astype(jnp.float32)
    sigma = 1.0 / (1.0 + jnp.exp(-act_a))
    gate_part = hidden_grad * act_b * sigma * (1.0 + act_a * (1.0 - sigma))
    up_part = hidden_grad * act_a * sigma
    out_ref[:, :hidden] = gate_part.astype(out_ref.dtype)
    out_ref[:, hidden:] = up_part.astype(out_ref.dtype)


def activation(gate_pre, up_pre, c, partials):
    part, hidden = partials[0].shape
    saved = pl.BlockSpec((part, hidden), lambda i: (c, 0))
    return pl.pallas_call(
        activation_kernel,
        out_shape=jax.ShapeDtypeStruct((part, 2 * hidden), jnp.bfloat16),
        grid=(1,),
        in_specs=[saved, saved] + [pl.BlockSpec((part, hidden), lambda i: (0, 0))] * len(partials),
        out_specs=pl.BlockSpec((part, 2 * hidden), lambda i: (0, 0)),
        compiler_params=params(),
        cost_estimate=FREE,
        name="activation",
    )(gate_pre, up_pre, *partials)


def second_kernel(n, me_ref, dense_ref, gate_ref, up_ref, router_ref, *refs):
    *block_refs, out_ref, held = refs
    chips = n // 2
    hidden = gate_ref.shape[1]

    @pl.when(pl.program_id(0) == 0)
    def _():
        me = me_ref[0]
        chip, core = me // 2, lax.rem(me, 2)
        for step in range(chips):
            there = lax.rem(chip - step + chips, chips) * 2
            held[there + core] = block_refs[2 * step][...]
            held[there + 1 - core] = block_refs[2 * step + 1][...]

    both = held[...].reshape(-1, 2 * hidden)
    result = contract_last(both[:, :hidden], gate_ref[...])
    result = result + contract_last(both[:, hidden:], up_ref[...])
    dense = dense_ref[...].reshape(both.shape[0], -1)
    result = result + contract_last(dense, router_ref[...])
    out_ref[...] = result.astype(out_ref.dtype).reshape(out_ref.shape)


def second_product(me, blocks, c, dense, w_gate, w_up, w_router):
    n = len(blocks)
    part, both = blocks[0].shape
    width, hidden = w_gate.shape
    n_experts = w_router.shape[1]
    block = block_of(width, 256)
    return pl.pallas_call(
        functools.partial(second_kernel, n),
        out_shape=jax.ShapeDtypeStruct((n, part, width), jnp.bfloat16),
        grid_spec=pltpu.PrefetchScalarGridSpec(
            num_scalar_prefetch=1,
            grid=(width // block,),
            in_specs=[
                pl.BlockSpec((n, part, n_experts), lambda i, me: (0, c, 0)),
                pl.BlockSpec((block, hidden), lambda i, me: (i, 0)),
                pl.BlockSpec((block, hidden), lambda i, me: (i, 0)),
                pl.BlockSpec((block, n_experts), lambda i, me: (i, 0)),
            ]
            + [pl.BlockSpec((part, both), lambda i, me: (0, 0))] * n,
            out_specs=pl.BlockSpec((n, part, block), lambda i, me: (0, 0, i)),
            scratch_shapes=[pltpu.VMEM((n, part, both), jnp.bfloat16)],
        ),
        compiler_params=params(),
        cost_estimate=FREE,
        name="second_product",
    )(me, dense, w_gate, w_up, w_router, *blocks)


def shards(
    upstream,
    shared_down,
    shared_gate,
    shared_up,
    router_weight,
    gate_pre,
    up_pre,
    gate_grad,
    gate_scores,
    expert_ids,
):
    n = lax.axis_size("expert")
    chips = n // 2
    me = lax.axis_index("expert").astype(jnp.int32).reshape(1)
    tokens, width = upstream.shape[1:]
    rows = tokens // n
    chunks = min(CHUNKS, rows // 16)
    part = rows // chunks
    grads = upstream.reshape(n, rows, width)
    arrived = [back_one(take_rows(grads, c, part)) for c in range(chunks)]
    dense = routed_grad(gate_grad[0], gate_scores[0], expert_ids[0], router_weight.shape[2])
    dense = dense.reshape(n, rows, -1)

    def partial_sums(c):
        own, *others = first_product(me, arrived[c], shared_down[0])
        return [own] + [to_expert(x, j + 1) for j, x in enumerate(others)]

    arrived[0], dense = in_order(arrived[0], dense)
    own = activation(gate_pre[0], up_pre[0], 0, partial_sums(0))
    out, sent = None, []
    for c in range(chunks):
        near = [own] + [to_expert(own, 2 * step) for step in range(1, chips)]
        far = [to_other_core(own)]
        if c + 1 < chunks:
            arrived[c + 1], own = in_order(arrived[c + 1], own)
            partials = partial_sums(c + 1)
            partials[0], near[-1] = in_order(partials[0], near[-1])
        far += [to_other_core(x) for x in near[1:]]
        if c >= 2:
            far[-1], out = in_order(far[-1], out)
        blocks = [x for pair in zip(near, far) for x in pair]
        result = second_product(
            me, blocks, c, dense, shared_gate[0], shared_up[0], router_weight[0]
        )
        if c + 1 < chunks:
            partials[0], result = in_order(partials[0], result)
            own = activation(gate_pre[0], up_pre[0], c + 1, partials)
        sent.append(back_one(result))
        if c >= 1:
            out = put_rows(out, sent[c - 1], c - 1, rows)
    out = put_rows(out, sent[-1], chunks - 1, rows)
    return out.reshape(1, tokens, width)


def solution(mesh):
    in_specs = (
        P("pipe", None, "expert"),
        P("pipe", None, "expert"),
        P("pipe", "expert", None),
        P("pipe", "expert", None),
        P("pipe", "expert", None),
        P("pipe", "expert", None),
        P("pipe", "expert", None),
        P("pipe", None, None),
        P("pipe", None, None),
        P("pipe", None, None),
    )
    out_specs = P("pipe", None, "expert")
    return jax.shard_map(shards, mesh=mesh, in_specs=in_specs, out_specs=out_specs, check_vma=False)
```

```python
import functools

import jax
import jax.numpy as jnp
from jax import lax
from jax.experimental import pallas as pl
from jax.experimental.pallas import tpu as pltpu
from jax.sharding import PartitionSpec as P

CHUNKS = 4
START = {2: 0, 3: 1}
WAIT = {("act", 3): (0,), ("mm2", 3): (1,), ("out", 2): (0,), ("out", 3): (1,)}
FREE = pl.CostEstimate(flops=0, bytes_accessed=0, transcendentals=0)


def params(**kwargs):
    return pltpu.CompilerParams(vmem_limit_bytes=48 * 1024 * 1024, **kwargs)


def block_of(size, most):
    fits = [b for b in range(128, min(size, most) + 1, 128) if size % b == 0]
    return fits[-1] if fits else size


def back_one(x):
    length = lax.axis_size("pipe")
    return lax.ppermute(x, "pipe", [(i, (i - 1) % length) for i in range(length)])


def to_expert(x, by):
    n = lax.axis_size("expert")
    return lax.ppermute(x, "expert", [(i, (i + by) % n) for i in range(n)])


def to_other_core(x):
    n = lax.axis_size("expert")
    return lax.ppermute(x, "expert", [(i, i ^ 1) for i in range(n)])


def in_order(later, earlier):
    return lax.optimization_barrier((later, earlier))


def contract_last(left, right):
    return lax.dot_general(
        left, right, (((1,), (1,)), ((), ())), preferred_element_type=jnp.float32
    )


def routed_kernel(grad_ref, score_ref, chosen_ref, out_ref):
    grad, scores, chosen = grad_ref[...], score_ref[...], chosen_ref[...]
    total = jnp.sum(scores, axis=-1, keepdims=True)
    mixed = jnp.sum(grad * scores, axis=-1, keepdims=True)
    logit_grad = 2.5 * (grad - mixed / total) / total * scores * (1.0 - scores)
    columns = lax.broadcasted_iota(jnp.int32, out_ref.shape, 1)
    dense = jnp.zeros(out_ref.shape, jnp.float32)
    for slot in range(grad.shape[1]):
        here = chosen[:, slot : slot + 1] == columns
        dense = dense + jnp.where(here, logit_grad[:, slot : slot + 1], 0.0)
    out_ref[...] = dense.astype(out_ref.dtype)


def routed_grad(grad, scores, chosen, n_experts):
    tokens, top = grad.shape
    block = min(tokens, 128)
    spec = pl.BlockSpec((block, top), lambda i: (i, 0))
    return pl.pallas_call(
        routed_kernel,
        out_shape=jax.ShapeDtypeStruct((tokens, n_experts), jnp.bfloat16),
        grid=(tokens // block,),
        in_specs=[spec, spec, spec],
        out_specs=pl.BlockSpec((block, n_experts), lambda i: (i, 0)),
        cost_estimate=FREE,
        name="routed_grad",
    )(grad, scores, chosen)


def first_kernel(n, me_ref, rows_ref, weight_ref, *out_refs):
    me = me_ref[0]
    part = rows_ref.shape[1]
    left = jnp.concatenate([rows_ref[lax.rem(me + j, n)] for j in range(n)], axis=0)
    product = contract_last(left, weight_ref[...]).astype(jnp.bfloat16)
    for j in range(n):
        out_refs[j][...] = product[j * part : (j + 1) * part]


def first_product(me, rows, weight):
    n, part, width = rows.shape
    hidden = weight.shape[0]
    block = block_of(hidden, 256)
    return pl.pallas_call(
        functools.partial(first_kernel, n),
        out_shape=[jax.ShapeDtypeStruct((part, hidden), jnp.bfloat16)] * n,
        grid_spec=pltpu.PrefetchScalarGridSpec(
            num_scalar_prefetch=1,
            grid=(hidden // block,),
            in_specs=[
                pl.BlockSpec((n, part, width), lambda i, me: (0, 0, 0)),
                pl.BlockSpec((block, width), lambda i, me: (i, 0)),
            ],
            out_specs=[pl.BlockSpec((part, block), lambda i, me: (0, i))] * n,
        ),
        compiler_params=params(),
        cost_estimate=FREE,
        name="first_product",
    )(me, rows, weight)


def activation_kernel(gate_ref, up_ref, *refs):
    *part_refs, out_ref = refs
    hidden = gate_ref.shape[1]
    hidden_grad = part_refs[0][...].astype(jnp.float32)
    for ref in part_refs[1:]:
        hidden_grad = hidden_grad + ref[...].astype(jnp.float32)
    act_a = gate_ref[...].astype(jnp.float32)
    act_b = up_ref[...].astype(jnp.float32)
    sigma = 1.0 / (1.0 + jnp.exp(-act_a))
    gate_part = hidden_grad * act_b * sigma * (1.0 + act_a * (1.0 - sigma))
    up_part = hidden_grad * act_a * sigma
    out_ref[:, :hidden] = gate_part.astype(out_ref.dtype)
    out_ref[:, hidden:] = up_part.astype(out_ref.dtype)


def activation(gate_pre, up_pre, c, partials):
    part, hidden = partials[0].shape
    saved = pl.BlockSpec((part, hidden), lambda i: (c, 0))
    return pl.pallas_call(
        activation_kernel,
        out_shape=jax.ShapeDtypeStruct((part, 2 * hidden), jnp.bfloat16),
        grid=(1,),
        in_specs=[saved, saved] + [pl.BlockSpec((part, hidden), lambda i: (0, 0))] * len(partials),
        out_specs=pl.BlockSpec((part, 2 * hidden), lambda i: (0, 0)),
        compiler_params=params(),
        cost_estimate=FREE,
        name="activation",
    )(gate_pre, up_pre, *partials)


def second_kernel(n, me_ref, dense_ref, gate_ref, up_ref, router_ref, *refs):
    *block_refs, out_ref, held = refs
    chips = n // 2
    hidden = gate_ref.shape[1]

    @pl.when(pl.program_id(0) == 0)
    def _():
        me = me_ref[0]
        chip, core = me // 2, lax.rem(me, 2)
        for step in range(chips):
            there = lax.rem(chip - step + chips, chips) * 2
            held[there + core] = block_refs[2 * step][...]
            held[there + 1 - core] = block_refs[2 * step + 1][...]

    both = held[...].reshape(-1, 2 * hidden)
    result = contract_last(both[:, :hidden], gate_ref[...])
    result = result + contract_last(both[:, hidden:], up_ref[...])
    dense = dense_ref[...].reshape(both.shape[0], -1)
    result = result + contract_last(dense, router_ref[...])
    out_ref[...] = result.astype(out_ref.dtype).reshape(out_ref.shape)


def second_product(me, blocks, c, dense, w_gate, w_up, w_router):
    n = len(blocks)
    part, both = blocks[0].shape
    width, hidden = w_gate.shape
    n_experts = w_router.shape[1]
    block = block_of(width, 256)
    return pl.pallas_call(
        functools.partial(second_kernel, n),
        out_shape=jax.ShapeDtypeStruct((n, part, width), jnp.bfloat16),
        grid_spec=pltpu.PrefetchScalarGridSpec(
            num_scalar_prefetch=1,
            grid=(width // block,),
            in_specs=[
                pl.BlockSpec((n, part, n_experts), lambda i, me: (0, c, 0)),
                pl.BlockSpec((block, hidden), lambda i, me: (i, 0)),
                pl.BlockSpec((block, hidden), lambda i, me: (i, 0)),
                pl.BlockSpec((block, n_experts), lambda i, me: (i, 0)),
            ]
            + [pl.BlockSpec((part, both), lambda i, me: (0, 0))] * n,
            out_specs=pl.BlockSpec((n, part, block), lambda i, me: (0, 0, i)),
            scratch_shapes=[pltpu.VMEM((n, part, both), jnp.bfloat16)],
        ),
        compiler_params=params(),
        cost_estimate=FREE,
        name="second_product",
    )(me, dense, w_gate, w_up, w_router, *blocks)


def shards(
    upstream,
    shared_down,
    shared_gate,
    shared_up,
    router_weight,
    gate_pre,
    up_pre,
    gate_grad,
    gate_scores,
    expert_ids,
):
    n = lax.axis_size("expert")
    chips = n // 2
    me = lax.axis_index("expert").astype(jnp.int32).reshape(1)
    tokens, width = upstream.shape[1:]
    rows = tokens // n
    chunks = min(CHUNKS, rows // 16)
    part = rows // chunks
    grads = upstream.reshape(n, rows, width)
    arrived, sent = [], []
    dense = routed_grad(gate_grad[0], gate_scores[0], expert_ids[0], router_weight.shape[2])
    for c in range(chunks):
        source = grads
        if c in START and START[c] < c:
            source, arrived[START[c]] = in_order(source, arrived[START[c]])
        elif c > 0:
            source, dense = in_order(source, dense)
        arrived.append(back_one(source[:, c * part : (c + 1) * part]))
    dense = dense.reshape(n, rows, -1)

    def at(point, c, x):
        for p in WAIT.get((point, c), ()):
            x, sent[p] = in_order(x, sent[p])
        return x

    def partial_sums(c):
        own, *others = first_product(me, arrived[c], shared_down[0])
        others[0] = at("rs", c, others[0])
        return [own] + [to_expert(x, j + 1) for j, x in enumerate(others)]

    arrived[0], dense = in_order(arrived[0], dense)
    own = activation(gate_pre[0], up_pre[0], 0, partial_sums(0))
    for c in range(chunks):
        own = at("agy", c, own)
        near = [own] + [to_expert(own, 2 * step) for step in range(1, chips)]
        far = [to_other_core(own)]
        if c + 1 < chunks:
            arrived[c + 1], own = in_order(arrived[c + 1], own)
            partials = partial_sums(c + 1)
            partials[0], near[-1] = in_order(partials[0], near[-1])
        near[-1] = at("agc", c, near[-1])
        far += [to_other_core(x) for x in near[1:]]
        far[-1] = at("mm2", c, far[-1])
        blocks = [x for pair in zip(near, far) for x in pair]
        result = second_product(
            me, blocks, c, dense, shared_gate[0], shared_up[0], router_weight[0]
        )
        if c + 1 < chunks:
            partials[0], result = in_order(partials[0], result)
            partials[0] = at("act", c + 1, partials[0])
            own = activation(gate_pre[0], up_pre[0], c + 1, partials)
        result = at("out", c, result)
        sent.append(back_one(result))
    out = jnp.zeros((n, rows, width), jnp.bfloat16)
    for c in range(chunks):
        out = lax.dynamic_update_slice(out, sent[c], (0, c * part, 0))
    return out.reshape(1, tokens, width)


def solution(mesh):
    in_specs = (
        P("pipe", None, "expert"),
        P("pipe", None, "expert"),
        P("pipe", "expert", None),
        P("pipe", "expert", None),
        P("pipe", "expert", None),
        P("pipe", "expert", None),
        P("pipe", "expert", None),
        P("pipe", None, None),
        P("pipe", None, None),
        P("pipe", None, None),
    )
    out_specs = P("pipe", None, "expert")
    return jax.shard_map(shards, mesh=mesh, in_specs=in_specs, out_specs=out_specs, check_vma=False)
```

```python
import functools

import jax
import jax.numpy as jnp
from jax import lax
from jax.experimental import pallas as pl
from jax.experimental.pallas import tpu as pltpu
from jax.sharding import PartitionSpec as P

CHUNKS = 4
IN_FLIGHT = 2
NEED = {("act", 1): (2,), ("act", 2): (3,)}
WAIT = {("act", 3): (0,), ("mm2", 3): (1,), ("out", 2): (0,), ("out", 3): (1,)}
FREE = pl.CostEstimate(flops=0, bytes_accessed=0, transcendentals=0)


def params(**kwargs):
    return pltpu.CompilerParams(vmem_limit_bytes=48 * 1024 * 1024, **kwargs)


def block_of(size, most):
    fits = [b for b in range(128, min(size, most) + 1, 128) if size % b == 0]
    return fits[-1] if fits else size


def back_one(x):
    length = lax.axis_size("pipe")
    return lax.ppermute(x, "pipe", [(i, (i - 1) % length) for i in range(length)])


def to_expert(x, by):
    n = lax.axis_size("expert")
    return lax.ppermute(x, "expert", [(i, (i + by) % n) for i in range(n)])


def to_other_core(x):
    n = lax.axis_size("expert")
    return lax.ppermute(x, "expert", [(i, i ^ 1) for i in range(n)])


def in_hbm(x):
    return pltpu.with_memory_space_constraint(x, pltpu.HBM)


def in_order(later, earlier):
    return lax.optimization_barrier((later, earlier))


def contract_last(left, right):
    return lax.dot_general(
        left, right, (((1,), (1,)), ((), ())), preferred_element_type=jnp.float32
    )


def take_kernel(c, pieces, source, target, sems):
    n, part, _ = target.shape
    step = part // pieces
    copies = []
    for i in range(n):
        for k in range(pieces):
            copy = pltpu.make_async_copy(
                source.at[i, pl.ds(c * part + k * step, step)],
                target.at[i, pl.ds(k * step, step)],
                sems.at[i, k],
            )
            copy.start()
            copies.append(copy)
    for copy in copies:
        copy.wait()


def put_kernel(c, pieces, source, old, target, sems):
    del old
    n, part, _ = source.shape
    step = part // pieces
    copies = []
    for i in range(n):
        for k in range(pieces):
            copy = pltpu.make_async_copy(
                source.at[i, pl.ds(k * step, step)],
                target.at[i, pl.ds(c * part + k * step, step)],
                sems.at[i, k],
            )
            copy.start()
            copies.append(copy)
    for copy in copies:
        copy.wait()


def pieces_of(part):
    return 2 if part % 32 == 0 else 1


def take_rows(array, c, part):
    n, _, width = array.shape
    pieces = pieces_of(part)
    return pl.pallas_call(
        functools.partial(take_kernel, c, pieces),
        out_shape=pltpu.VMEM((n, part, width), array.dtype),
        in_specs=[pl.BlockSpec(memory_space=pltpu.HBM)],
        out_specs=pl.BlockSpec(memory_space=pltpu.VMEM),
        scratch_shapes=[pltpu.SemaphoreType.DMA((n, pieces))],
        cost_estimate=FREE,
        name="take_rows",
    )(in_hbm(array))


def put_rows(out, piece, c):
    n, part, _ = piece.shape
    pieces = pieces_of(part)
    return pl.pallas_call(
        functools.partial(put_kernel, c, pieces),
        out_shape=jax.ShapeDtypeStruct(out.shape, out.dtype),
        in_specs=[pl.BlockSpec(memory_space=pltpu.VMEM), pl.BlockSpec(memory_space=pltpu.HBM)],
        out_specs=pl.BlockSpec(memory_space=pltpu.HBM),
        scratch_shapes=[pltpu.SemaphoreType.DMA((n, pieces))],
        input_output_aliases={1: 0},
        cost_estimate=FREE,
        name="put_rows",
    )(pltpu.with_memory_space_constraint(piece, pltpu.VMEM), out)


def routed_kernel(grad_ref, score_ref, chosen_ref, out_ref):
    grad, scores, chosen = grad_ref[...], score_ref[...], chosen_ref[...]
    total = jnp.sum(scores, axis=0, keepdims=True)
    mixed = jnp.sum(grad * scores, axis=0, keepdims=True)
    logit_grad = 2.5 * (grad - mixed / total) / total * scores * (1.0 - scores)
    experts = lax.broadcasted_iota(jnp.int32, out_ref.shape[::-1], 0)
    dense = jnp.zeros(experts.shape, jnp.float32)
    for slot in range(grad.shape[0]):
        here = chosen[slot : slot + 1] == experts
        dense = dense + jnp.where(here, logit_grad[slot : slot + 1], 0.0)
    out_ref[...] = dense.T.astype(out_ref.dtype)


def routed_grad(grad, scores, chosen, n_experts):
    tokens, top = grad.shape
    block = block_of(tokens, 128)
    spec = pl.BlockSpec((top, block), lambda i: (0, i))
    return pl.pallas_call(
        routed_kernel,
        out_shape=jax.ShapeDtypeStruct((tokens, n_experts), jnp.bfloat16),
        grid=(tokens // block,),
        in_specs=[spec, spec, spec],
        out_specs=pl.BlockSpec((block, n_experts), lambda i: (i, 0)),
        cost_estimate=FREE,
        name="routed_grad",
    )(in_hbm(grad.T), in_hbm(scores.T), in_hbm(chosen.T))


def first_kernel(n, me_ref, rows_ref, weight_ref, *out_refs):
    me = me_ref[0]
    part = rows_ref.shape[1]
    left = jnp.concatenate([rows_ref[lax.rem(me + j, n)] for j in range(n)], axis=0)
    product = contract_last(left, weight_ref[...]).astype(jnp.bfloat16)
    for j in range(n):
        out_refs[j][...] = product[j * part : (j + 1) * part]


def first_product(me, rows, weight, late):
    n, part, width = rows.shape
    hidden = weight.shape[0]
    block = block_of(hidden, 256)
    return pl.pallas_call(
        functools.partial(first_kernel, n),
        out_shape=[jax.ShapeDtypeStruct((part, hidden), jnp.bfloat16)] * n,
        grid_spec=pltpu.PrefetchScalarGridSpec(
            num_scalar_prefetch=1,
            grid=(hidden // block,),
            in_specs=[
                pl.BlockSpec((n, part, width), lambda i, me: (0, 0, 0)),
                pl.BlockSpec((block, width), lambda i, me: (i, 0)),
            ],
            out_specs=[pl.BlockSpec((part, block), lambda i, me: (0, i))] * n,
        ),
        compiler_params=params(),
        cost_estimate=FREE,
        name="first_product",
    )(me, rows, weight if late else in_hbm(weight))


def activation_kernel(gate_ref, up_ref, *refs):
    *part_refs, out_ref = refs
    hidden = gate_ref.shape[1]
    hidden_grad = part_refs[0][...].astype(jnp.float32)
    for ref in part_refs[1:]:
        hidden_grad = hidden_grad + ref[...].astype(jnp.float32)
    act_a = gate_ref[...].astype(jnp.float32)
    act_b = up_ref[...].astype(jnp.float32)
    sigma = 1.0 / (1.0 + jnp.exp(-act_a))
    gate_part = hidden_grad * act_b * sigma * (1.0 + act_a * (1.0 - sigma))
    up_part = hidden_grad * act_a * sigma
    out_ref[:, :hidden] = gate_part.astype(out_ref.dtype)
    out_ref[:, hidden:] = up_part.astype(out_ref.dtype)


def activation(gate_pre, up_pre, c, partials):
    part, hidden = partials[0].shape
    saved = pl.BlockSpec((part, hidden), lambda i: (c, 0))
    return pl.pallas_call(
        activation_kernel,
        out_shape=jax.ShapeDtypeStruct((part, 2 * hidden), jnp.bfloat16),
        grid=(1,),
        in_specs=[saved, saved] + [pl.BlockSpec((part, hidden), lambda i: (0, 0))] * len(partials),
        out_specs=pl.BlockSpec((part, 2 * hidden), lambda i: (0, 0)),
        compiler_params=params(),
        cost_estimate=FREE,
        name="activation",
    )(in_hbm(gate_pre), in_hbm(up_pre), *partials)


def second_kernel(n, me_ref, dense_ref, gate_ref, up_ref, router_ref, *refs):
    *block_refs, out_ref, held = refs
    chips = n // 2
    hidden = gate_ref.shape[1]

    @pl.when(pl.program_id(0) == 0)
    def _():
        me = me_ref[0]
        chip, core = me // 2, lax.rem(me, 2)
        for step in range(chips):
            there = lax.rem(chip - step + chips, chips) * 2
            held[there + core] = block_refs[2 * step][...]
            held[there + 1 - core] = block_refs[2 * step + 1][...]

    both = held[...].reshape(-1, 2 * hidden)
    result = contract_last(both[:, :hidden], gate_ref[...])
    result = result + contract_last(both[:, hidden:], up_ref[...])
    dense = dense_ref[...].reshape(both.shape[0], -1)
    result = result + contract_last(dense, router_ref[...])
    out_ref[...] = result.astype(out_ref.dtype).reshape(out_ref.shape)


def second_product(me, blocks, c, dense, w_gate, w_up, w_router):
    n = len(blocks)
    part, both = blocks[0].shape
    width, hidden = w_gate.shape
    n_experts = w_router.shape[1]
    block = block_of(width, 256)
    return pl.pallas_call(
        functools.partial(second_kernel, n),
        out_shape=jax.ShapeDtypeStruct((n, part, width), jnp.bfloat16),
        grid_spec=pltpu.PrefetchScalarGridSpec(
            num_scalar_prefetch=1,
            grid=(width // block,),
            in_specs=[
                pl.BlockSpec((n, part, n_experts), lambda i, me: (0, c, 0)),
                pl.BlockSpec((block, hidden), lambda i, me: (i, 0)),
                pl.BlockSpec((block, hidden), lambda i, me: (i, 0)),
                pl.BlockSpec((block, n_experts), lambda i, me: (i, 0)),
            ]
            + [pl.BlockSpec((part, both), lambda i, me: (0, 0))] * n,
            out_specs=pl.BlockSpec((n, part, block), lambda i, me: (0, 0, i)),
            scratch_shapes=[pltpu.VMEM((n, part, both), jnp.bfloat16)],
        ),
        compiler_params=params(),
        cost_estimate=FREE,
        name="second_product",
    )(me, dense, w_gate, w_up, w_router, *blocks)


def shards(
    upstream,
    shared_down,
    shared_gate,
    shared_up,
    router_weight,
    gate_pre,
    up_pre,
    gate_grad,
    gate_scores,
    expert_ids,
):
    n = lax.axis_size("expert")
    chips = n // 2
    me = lax.axis_index("expert").astype(jnp.int32).reshape(1)
    tokens, width = upstream.shape[1:]
    rows = tokens // n
    chunks = min(CHUNKS, rows // 16)
    part = rows // chunks
    grads = upstream.reshape(n, rows, width)
    arrived, sent = [], []
    dense = routed_grad(gate_grad[0], gate_scores[0], expert_ids[0], router_weight.shape[2])
    for c in range(chunks):
        if c == 0:
            piece = take_rows(grads, c, part)
            grads, dense = in_order(grads, dense)
        else:
            piece = grads[:, c * part : (c + 1) * part]
        if c >= IN_FLIGHT:
            piece, arrived[c - IN_FLIGHT] = in_order(piece, arrived[c - IN_FLIGHT])
        arrived.append(back_one(piece))
    dense = dense.reshape(n, rows, -1)

    def at(point, c, x):
        for p in NEED.get((point, c), ()):
            x, arrived[p] = in_order(x, arrived[p])
        for p in WAIT.get((point, c), ()):
            x, sent[p] = in_order(x, sent[p])
        return x

    def partial_sums(c):
        own, *others = first_product(me, arrived[c], shared_down[0], c > 0)
        others[0] = at("rs", c, others[0])
        return [own] + [to_expert(x, j + 1) for j, x in enumerate(others)]

    arrived[0], dense = in_order(arrived[0], dense)
    own = activation(gate_pre[0], up_pre[0], 0, partial_sums(0))
    for c in range(chunks):
        own = at("agy", c, own)
        near = [own] + [to_expert(own, 2 * step) for step in range(1, chips)]
        far = [to_other_core(own)]
        if c + 1 < chunks:
            arrived[c + 1], own = in_order(arrived[c + 1], own)
            partials = partial_sums(c + 1)
            partials[0], near[-1] = in_order(partials[0], near[-1])
        near[-1] = at("agc", c, near[-1])
        far += [to_other_core(x) for x in near[1:]]
        far[-1] = at("mm2", c, far[-1])
        blocks = [x for pair in zip(near, far) for x in pair]
        result = second_product(
            me, blocks, c, dense, shared_gate[0], shared_up[0], router_weight[0]
        )
        if c + 1 < chunks:
            partials[0], result = in_order(partials[0], result)
            partials[0] = at("act", c + 1, partials[0])
            own = activation(gate_pre[0], up_pre[0], c + 1, partials)
        result = at("out", c, result)
        sent.append(back_one(result))
    out = jnp.zeros((n, rows, width), jnp.bfloat16)
    for c in range(chunks - 1):
        out = lax.dynamic_update_slice(out, sent[c], (0, c * part, 0))
    out = put_rows(out, sent[-1], chunks - 1)
    return out.reshape(1, tokens, width)


def solution(mesh):
    in_specs = (
        P("pipe", None, "expert"),
        P("pipe", None, "expert"),
        P("pipe", "expert", None),
        P("pipe", "expert", None),
        P("pipe", "expert", None),
        P("pipe", "expert", None),
        P("pipe", "expert", None),
        P("pipe", None, None),
        P("pipe", None, None),
        P("pipe", None, None),
    )
    out_specs = P("pipe", None, "expert")
    return jax.shard_map(shards, mesh=mesh, in_specs=in_specs, out_specs=out_specs, check_vma=False)
```

```python
import functools

import jax
import jax.numpy as jnp
from jax import lax
from jax.experimental import pallas as pl
from jax.experimental.pallas import tpu as pltpu
from jax.sharding import PartitionSpec as P

CHUNKS = 4
LAST = 16
IN_FLIGHT = 2
NEED = {("act", 1): (2,), ("act", 2): (3,)}
WAIT = {("act", 3): (0,), ("mm2", 3): (1,), ("out", 2): (0,), ("out", 3): (1,)}
FREE = pl.CostEstimate(flops=0, bytes_accessed=0, transcendentals=0)


def params(**kwargs):
    return pltpu.CompilerParams(vmem_limit_bytes=48 * 1024 * 1024, **kwargs)


def block_of(size, most):
    fits = [b for b in range(128, min(size, most) + 1, 128) if size % b == 0]
    return fits[-1] if fits else size


def back_one(x):
    length = lax.axis_size("pipe")
    return lax.ppermute(x, "pipe", [(i, (i - 1) % length) for i in range(length)])


def to_expert(x, by):
    n = lax.axis_size("expert")
    return lax.ppermute(x, "expert", [(i, (i + by) % n) for i in range(n)])


def to_other_core(x):
    n = lax.axis_size("expert")
    return lax.ppermute(x, "expert", [(i, i ^ 1) for i in range(n)])


def in_hbm(x):
    return pltpu.with_memory_space_constraint(x, pltpu.HBM)


def in_order(later, earlier):
    return lax.optimization_barrier((later, earlier))


def contract_last(left, right):
    return lax.dot_general(
        left, right, (((1,), (1,)), ((), ())), preferred_element_type=jnp.float32
    )


def take_kernel(start, source, target, sem):
    here = pl.ds(start, target.shape[1])
    copy = pltpu.make_async_copy(source.at[:, here], target, sem)
    copy.start()
    copy.wait()


def put_kernel(start, source, old, target, sem):
    del old
    here = pl.ds(start, source.shape[1])
    copy = pltpu.make_async_copy(source, target.at[:, here], sem)
    copy.start()
    copy.wait()


def take_rows(array, start, size):
    n, _, width = array.shape
    return pl.pallas_call(
        functools.partial(take_kernel, start),
        out_shape=pltpu.VMEM((n, size, width), array.dtype),
        in_specs=[pl.BlockSpec(memory_space=pltpu.HBM)],
        out_specs=pl.BlockSpec(memory_space=pltpu.VMEM),
        scratch_shapes=[pltpu.SemaphoreType.DMA],
        cost_estimate=FREE,
        name="take_rows",
    )(in_hbm(array))


def put_rows(out, piece, start):
    return pl.pallas_call(
        functools.partial(put_kernel, start),
        out_shape=jax.ShapeDtypeStruct(out.shape, out.dtype),
        in_specs=[pl.BlockSpec(memory_space=pltpu.VMEM), pl.BlockSpec(memory_space=pltpu.HBM)],
        out_specs=pl.BlockSpec(memory_space=pltpu.HBM),
        scratch_shapes=[pltpu.SemaphoreType.DMA],
        input_output_aliases={1: 0},
        cost_estimate=FREE,
        name="put_rows",
    )(pltpu.with_memory_space_constraint(piece, pltpu.VMEM), out)


def routed_kernel(grad_ref, score_ref, chosen_ref, out_ref):
    grad, scores, chosen = grad_ref[...], score_ref[...], chosen_ref[...]
    total = jnp.sum(scores, axis=0, keepdims=True)
    mixed = jnp.sum(grad * scores, axis=0, keepdims=True)
    logit_grad = 2.5 * (grad - mixed / total) / total * scores * (1.0 - scores)
    experts = lax.broadcasted_iota(jnp.int32, out_ref.shape[::-1], 0)
    dense = jnp.zeros(experts.shape, jnp.float32)
    for slot in range(grad.shape[0]):
        here = chosen[slot : slot + 1] == experts
        dense = dense + jnp.where(here, logit_grad[slot : slot + 1], 0.0)
    out_ref[...] = dense.T.astype(out_ref.dtype)


def routed_grad(grad, scores, chosen, n_experts):
    tokens, top = grad.shape
    block = block_of(tokens, 128)
    spec = pl.BlockSpec((top, block), lambda i: (0, i))
    return pl.pallas_call(
        routed_kernel,
        out_shape=jax.ShapeDtypeStruct((tokens, n_experts), jnp.bfloat16),
        grid=(tokens // block,),
        in_specs=[spec, spec, spec],
        out_specs=pl.BlockSpec((block, n_experts), lambda i: (i, 0)),
        cost_estimate=FREE,
        name="routed_grad",
    )(in_hbm(grad.T), in_hbm(scores.T), in_hbm(chosen.T))


def first_kernel(n, me_ref, rows_ref, weight_ref, *out_refs):
    me = me_ref[0]
    part = rows_ref.shape[1]
    left = jnp.concatenate([rows_ref[lax.rem(me + j, n)] for j in range(n)], axis=0)
    product = contract_last(left, weight_ref[...]).astype(jnp.bfloat16)
    for j in range(n):
        out_refs[j][...] = product[j * part : (j + 1) * part]


def first_product(me, rows, weight, late):
    n, part, width = rows.shape
    hidden = weight.shape[0]
    block = block_of(hidden, 256)
    return pl.pallas_call(
        functools.partial(first_kernel, n),
        out_shape=[jax.ShapeDtypeStruct((part, hidden), jnp.bfloat16)] * n,
        grid_spec=pltpu.PrefetchScalarGridSpec(
            num_scalar_prefetch=1,
            grid=(hidden // block,),
            in_specs=[
                pl.BlockSpec((n, part, width), lambda i, me: (0, 0, 0)),
                pl.BlockSpec((block, width), lambda i, me: (i, 0)),
            ],
            out_specs=[pl.BlockSpec((part, block), lambda i, me: (0, i))] * n,
        ),
        compiler_params=params(),
        cost_estimate=FREE,
        name="first_product",
    )(me, rows, weight if late else in_hbm(weight))


def activation_kernel(gate_ref, up_ref, *refs):
    *part_refs, out_ref = refs
    hidden = gate_ref.shape[1]
    hidden_grad = part_refs[0][...].astype(jnp.float32)
    for ref in part_refs[1:]:
        hidden_grad = hidden_grad + ref[...].astype(jnp.float32)
    act_a = gate_ref[...].astype(jnp.float32)
    act_b = up_ref[...].astype(jnp.float32)
    sigma = 1.0 / (1.0 + jnp.exp(-act_a))
    gate_part = hidden_grad * act_b * sigma * (1.0 + act_a * (1.0 - sigma))
    up_part = hidden_grad * act_a * sigma
    out_ref[:, :hidden] = gate_part.astype(out_ref.dtype)
    out_ref[:, hidden:] = up_part.astype(out_ref.dtype)


def activation(gate_pre, up_pre, c, partials):
    part, hidden = partials[0].shape
    saved = pl.BlockSpec((part, hidden), lambda i: (c, 0))
    return pl.pallas_call(
        activation_kernel,
        out_shape=jax.ShapeDtypeStruct((part, 2 * hidden), jnp.bfloat16),
        grid=(1,),
        in_specs=[saved, saved] + [pl.BlockSpec((part, hidden), lambda i: (0, 0))] * len(partials),
        out_specs=pl.BlockSpec((part, 2 * hidden), lambda i: (0, 0)),
        compiler_params=params(),
        cost_estimate=FREE,
        name="activation",
    )(in_hbm(gate_pre), in_hbm(up_pre), *partials)


def second_kernel(n, me_ref, dense_ref, gate_ref, up_ref, router_ref, *refs):
    block_refs, out_refs, held = refs[:n], refs[n:-1], refs[-1]
    chips = n // 2
    hidden = gate_ref.shape[1]

    @pl.when(pl.program_id(0) == 0)
    def _():
        me = me_ref[0]
        chip, core = me // 2, lax.rem(me, 2)
        for step in range(chips):
            there = lax.rem(chip - step + chips, chips) * 2
            held[there + core] = block_refs[2 * step][...]
            held[there + 1 - core] = block_refs[2 * step + 1][...]

    both = held[...].reshape(-1, 2 * hidden)
    result = contract_last(both[:, :hidden], gate_ref[...])
    result = result + contract_last(both[:, hidden:], up_ref[...])
    dense = dense_ref[...].reshape(both.shape[0], -1)
    result = result + contract_last(dense, router_ref[...])
    result = result.astype(jnp.bfloat16).reshape(n, held.shape[1], -1)
    first = 0
    for out_ref in out_refs:
        size = out_ref.shape[1]
        out_ref[...] = result[:, first : first + size]
        first += size


def second_product(me, blocks, c, dense, w_gate, w_up, w_router, sizes):
    n = len(blocks)
    part, both = blocks[0].shape
    width, hidden = w_gate.shape
    n_experts = w_router.shape[1]
    block = block_of(width, 256)
    return pl.pallas_call(
        functools.partial(second_kernel, n),
        out_shape=[jax.ShapeDtypeStruct((n, size, width), jnp.bfloat16) for size in sizes],
        grid_spec=pltpu.PrefetchScalarGridSpec(
            num_scalar_prefetch=1,
            grid=(width // block,),
            in_specs=[
                pl.BlockSpec((n, part, n_experts), lambda i, me: (0, c, 0)),
                pl.BlockSpec((block, hidden), lambda i, me: (i, 0)),
                pl.BlockSpec((block, hidden), lambda i, me: (i, 0)),
                pl.BlockSpec((block, n_experts), lambda i, me: (i, 0)),
            ]
            + [pl.BlockSpec((part, both), lambda i, me: (0, 0))] * n,
            out_specs=[pl.BlockSpec((n, size, block), lambda i, me: (0, 0, i)) for size in sizes],
            scratch_shapes=[pltpu.VMEM((n, part, both), jnp.bfloat16)],
        ),
        compiler_params=params(),
        cost_estimate=FREE,
        name="second_product",
    )(me, dense, w_gate, w_up, w_router, *blocks)


def shards(
    upstream,
    shared_down,
    shared_gate,
    shared_up,
    router_weight,
    gate_pre,
    up_pre,
    gate_grad,
    gate_scores,
    expert_ids,
):
    n = lax.axis_size("expert")
    chips = n // 2
    me = lax.axis_index("expert").astype(jnp.int32).reshape(1)
    tokens, width = upstream.shape[1:]
    rows = tokens // n
    chunks = min(CHUNKS, rows // 16)
    part = rows // chunks
    grads = upstream.reshape(n, rows, width)
    arrived, sent = [], []
    dense = routed_grad(gate_grad[0], gate_scores[0], expert_ids[0], router_weight.shape[2])
    for c in range(chunks):
        if c == 0:
            piece = take_rows(grads, 0, part)
            grads, dense = in_order(grads, dense)
        else:
            piece = grads[:, c * part : (c + 1) * part]
        if c >= IN_FLIGHT:
            piece, arrived[c - IN_FLIGHT] = in_order(piece, arrived[c - IN_FLIGHT])
        arrived.append(back_one(piece))
    dense = dense.reshape(n, rows, -1)

    def at(point, c, x):
        for p in NEED.get((point, c), ()):
            x, arrived[p] = in_order(x, arrived[p])
        for p in WAIT.get((point, c), ()):
            x, sent[p] = in_order(x, sent[p])
        return x

    def partial_sums(c):
        own, *others = first_product(me, arrived[c], shared_down[0], c > 0)
        others[0] = at("rs", c, others[0])
        return [own] + [to_expert(x, j + 1) for j, x in enumerate(others)]

    arrived[0], dense = in_order(arrived[0], dense)
    own = activation(gate_pre[0], up_pre[0], 0, partial_sums(0))
    for c in range(chunks):
        own = at("agy", c, own)
        near = [own] + [to_expert(own, 2 * step) for step in range(1, chips)]
        far = [to_other_core(own)]
        if c + 1 < chunks:
            arrived[c + 1], own = in_order(arrived[c + 1], own)
            partials = partial_sums(c + 1)
            partials[0], near[-1] = in_order(partials[0], near[-1])
        near[-1] = at("agc", c, near[-1])
        far += [to_other_core(x) for x in near[1:]]
        far[-1] = at("mm2", c, far[-1])
        blocks = [x for pair in zip(near, far) for x in pair]
        sizes = [part]
        if c + 1 == chunks and part > LAST:
            sizes = [part - LAST, LAST]
        result, *last = second_product(
            me, blocks, c, dense, shared_gate[0], shared_up[0], router_weight[0], sizes
        )
        if c + 1 < chunks:
            partials[0], result = in_order(partials[0], result)
            partials[0] = at("act", c + 1, partials[0])
            own = activation(gate_pre[0], up_pre[0], c + 1, partials)
        result = at("out", c, result)
        sent.append(back_one(result))
    out = jnp.zeros((n, rows, width), jnp.bfloat16)
    for c in range(chunks - 1):
        out = lax.dynamic_update_slice(out, sent[c], (0, c * part, 0))
    out = put_rows(out, sent[-1], (chunks - 1) * part)
    for piece in last:
        out = put_rows(out, back_one(piece), rows - LAST)
    return out.reshape(1, tokens, width)


def solution(mesh):
    in_specs = (
        P("pipe", None, "expert"),
        P("pipe", None, "expert"),
        P("pipe", "expert", None),
        P("pipe", "expert", None),
        P("pipe", "expert", None),
        P("pipe", "expert", None),
        P("pipe", "expert", None),
        P("pipe", None, None),
        P("pipe", None, None),
        P("pipe", None, None),
    )
    out_specs = P("pipe", None, "expert")
    return jax.shard_map(shards, mesh=mesh, in_specs=in_specs, out_specs=out_specs, check_vma=False)
```

```python
import functools

import jax
import jax.numpy as jnp
from jax import lax
from jax.experimental import pallas as pl
from jax.experimental.pallas import tpu as pltpu
from jax.sharding import PartitionSpec as P

PARTS = (3, 5, 4, 4)
LAST = 16
IN_FLIGHT = 2
NEED = {("act", 1): (2,), ("act", 2): (3,)}
WAIT = {("act", 3): (0,), ("mm2", 3): (1,), ("out", 2): (0,), ("out", 3): (1,)}
FREE = pl.CostEstimate(flops=0, bytes_accessed=0, transcendentals=0)


def params(**kwargs):
    return pltpu.CompilerParams(vmem_limit_bytes=48 * 1024 * 1024, **kwargs)


def cut(rows):
    if rows % 256 == 0:
        return [rows // 16 * share for share in PARTS]
    return [rows // 4] * 4 if rows % 64 == 0 else [rows]


def block_of(size, most):
    fits = [b for b in range(128, min(size, most) + 1, 128) if size % b == 0]
    return fits[-1] if fits else size


def back_one(x):
    length = lax.axis_size("pipe")
    return lax.ppermute(x, "pipe", [(i, (i - 1) % length) for i in range(length)])


def to_expert(x, by):
    n = lax.axis_size("expert")
    return lax.ppermute(x, "expert", [(i, (i + by) % n) for i in range(n)])


def to_other_core(x):
    n = lax.axis_size("expert")
    return lax.ppermute(x, "expert", [(i, i ^ 1) for i in range(n)])


def in_hbm(x):
    return pltpu.with_memory_space_constraint(x, pltpu.HBM)


def in_order(later, earlier):
    return lax.optimization_barrier((later, earlier))


def contract_last(left, right):
    return lax.dot_general(
        left, right, (((1,), (1,)), ((), ())), preferred_element_type=jnp.float32
    )


def take_kernel(start, source, target, sem):
    here = pl.ds(start, target.shape[1])
    copy = pltpu.make_async_copy(source.at[:, here], target, sem)
    copy.start()
    copy.wait()


def put_kernel(start, source, old, target, sem):
    del old
    here = pl.ds(start, source.shape[1])
    copy = pltpu.make_async_copy(source, target.at[:, here], sem)
    copy.start()
    copy.wait()


def take_rows(array, start, size):
    n, _, width = array.shape
    return pl.pallas_call(
        functools.partial(take_kernel, start),
        out_shape=pltpu.VMEM((n, size, width), array.dtype),
        in_specs=[pl.BlockSpec(memory_space=pltpu.HBM)],
        out_specs=pl.BlockSpec(memory_space=pltpu.VMEM),
        scratch_shapes=[pltpu.SemaphoreType.DMA],
        cost_estimate=FREE,
        name="take_rows",
    )(in_hbm(array))


def put_rows(out, piece, start):
    return pl.pallas_call(
        functools.partial(put_kernel, start),
        out_shape=jax.ShapeDtypeStruct(out.shape, out.dtype),
        in_specs=[pl.BlockSpec(memory_space=pltpu.VMEM), pl.BlockSpec(memory_space=pltpu.HBM)],
        out_specs=pl.BlockSpec(memory_space=pltpu.HBM),
        scratch_shapes=[pltpu.SemaphoreType.DMA],
        input_output_aliases={1: 0},
        cost_estimate=FREE,
        name="put_rows",
    )(pltpu.with_memory_space_constraint(piece, pltpu.VMEM), out)


def routed_kernel(grad_ref, score_ref, chosen_ref, out_ref):
    grad, scores, chosen = grad_ref[...], score_ref[...], chosen_ref[...]
    total = jnp.sum(scores, axis=0, keepdims=True)
    mixed = jnp.sum(grad * scores, axis=0, keepdims=True)
    logit_grad = 2.5 * (grad - mixed / total) / total * scores * (1.0 - scores)
    experts = lax.broadcasted_iota(jnp.int32, out_ref.shape[::-1], 0)
    dense = jnp.zeros(experts.shape, jnp.float32)
    for slot in range(grad.shape[0]):
        here = chosen[slot : slot + 1] == experts
        dense = dense + jnp.where(here, logit_grad[slot : slot + 1], 0.0)
    out_ref[...] = dense.T.astype(out_ref.dtype)


def routed_grad(grad, scores, chosen, n_experts):
    tokens, top = grad.shape
    block = block_of(tokens, 128)
    spec = pl.BlockSpec((top, block), lambda i: (0, i))
    return pl.pallas_call(
        routed_kernel,
        out_shape=jax.ShapeDtypeStruct((tokens, n_experts), jnp.bfloat16),
        grid=(tokens // block,),
        in_specs=[spec, spec, spec],
        out_specs=pl.BlockSpec((block, n_experts), lambda i: (i, 0)),
        cost_estimate=FREE,
        name="routed_grad",
    )(in_hbm(grad.T), in_hbm(scores.T), in_hbm(chosen.T))


def first_kernel(n, me_ref, rows_ref, weight_ref, *out_refs):
    me = me_ref[0]
    part = rows_ref.shape[1]
    left = jnp.concatenate([rows_ref[lax.rem(me + j, n)] for j in range(n)], axis=0)
    product = contract_last(left, weight_ref[...]).astype(jnp.bfloat16)
    for j in range(n):
        out_refs[j][...] = product[j * part : (j + 1) * part]


def first_product(me, rows, weight, late):
    n, part, width = rows.shape
    hidden = weight.shape[0]
    block = block_of(hidden, 256)
    return pl.pallas_call(
        functools.partial(first_kernel, n),
        out_shape=[jax.ShapeDtypeStruct((part, hidden), jnp.bfloat16)] * n,
        grid_spec=pltpu.PrefetchScalarGridSpec(
            num_scalar_prefetch=1,
            grid=(hidden // block,),
            in_specs=[
                pl.BlockSpec((n, part, width), lambda i, me: (0, 0, 0)),
                pl.BlockSpec((block, width), lambda i, me: (i, 0)),
            ],
            out_specs=[pl.BlockSpec((part, block), lambda i, me: (0, i))] * n,
        ),
        compiler_params=params(),
        cost_estimate=FREE,
        name="first_product",
    )(me, rows, weight if late else in_hbm(weight))


def activation_kernel(start, gate_ref, up_ref, *refs):
    *part_refs, out_ref = refs
    part, hidden = part_refs[0].shape
    here = slice(start, start + part)
    hidden_grad = part_refs[0][...].astype(jnp.float32)
    for ref in part_refs[1:]:
        hidden_grad = hidden_grad + ref[...].astype(jnp.float32)
    act_a = gate_ref[here].astype(jnp.float32)
    act_b = up_ref[here].astype(jnp.float32)
    sigma = 1.0 / (1.0 + jnp.exp(-act_a))
    gate_part = hidden_grad * act_b * sigma * (1.0 + act_a * (1.0 - sigma))
    up_part = hidden_grad * act_a * sigma
    out_ref[:, :hidden] = gate_part.astype(out_ref.dtype)
    out_ref[:, hidden:] = up_part.astype(out_ref.dtype)


def activation(gate_pre, up_pre, start, partials):
    part, hidden = partials[0].shape
    saved = pl.BlockSpec(gate_pre.shape, lambda i: (0, 0))
    return pl.pallas_call(
        functools.partial(activation_kernel, start),
        out_shape=jax.ShapeDtypeStruct((part, 2 * hidden), jnp.bfloat16),
        grid=(1,),
        in_specs=[saved, saved] + [pl.BlockSpec((part, hidden), lambda i: (0, 0))] * len(partials),
        out_specs=pl.BlockSpec((part, 2 * hidden), lambda i: (0, 0)),
        compiler_params=params(),
        cost_estimate=FREE,
        name="activation",
    )(in_hbm(gate_pre), in_hbm(up_pre), *partials)


def second_kernel(n, start, me_ref, dense_ref, gate_ref, up_ref, router_ref, *refs):
    block_refs, out_refs, held = refs[:n], refs[n:-1], refs[-1]
    chips = n // 2
    hidden = gate_ref.shape[1]

    @pl.when(pl.program_id(0) == 0)
    def _():
        me = me_ref[0]
        chip, core = me // 2, lax.rem(me, 2)
        for step in range(chips):
            there = lax.rem(chip - step + chips, chips) * 2
            held[there + core] = block_refs[2 * step][...]
            held[there + 1 - core] = block_refs[2 * step + 1][...]

    both = held[...].reshape(-1, 2 * hidden)
    result = contract_last(both[:, :hidden], gate_ref[...])
    result = result + contract_last(both[:, hidden:], up_ref[...])
    dense = dense_ref[:, start : start + held.shape[1]].reshape(both.shape[0], -1)
    result = result + contract_last(dense, router_ref[...])
    result = result.astype(jnp.bfloat16).reshape(n, held.shape[1], -1)
    first = 0
    for out_ref in out_refs:
        size = out_ref.shape[1]
        out_ref[...] = result[:, first : first + size]
        first += size


def second_product(me, blocks, start, dense, w_gate, w_up, w_router, sizes):
    n = len(blocks)
    part, both = blocks[0].shape
    width, hidden = w_gate.shape
    n_experts = w_router.shape[1]
    block = block_of(width, 256)
    return pl.pallas_call(
        functools.partial(second_kernel, n, start),
        out_shape=[jax.ShapeDtypeStruct((n, size, width), jnp.bfloat16) for size in sizes],
        grid_spec=pltpu.PrefetchScalarGridSpec(
            num_scalar_prefetch=1,
            grid=(width // block,),
            in_specs=[
                pl.BlockSpec(dense.shape, lambda i, me: (0, 0, 0)),
                pl.BlockSpec((block, hidden), lambda i, me: (i, 0)),
                pl.BlockSpec((block, hidden), lambda i, me: (i, 0)),
                pl.BlockSpec((block, n_experts), lambda i, me: (i, 0)),
            ]
            + [pl.BlockSpec((part, both), lambda i, me: (0, 0))] * n,
            out_specs=[pl.BlockSpec((n, size, block), lambda i, me: (0, 0, i)) for size in sizes],
            scratch_shapes=[pltpu.VMEM((n, part, both), jnp.bfloat16)],
        ),
        compiler_params=params(),
        cost_estimate=FREE,
        name="second_product",
    )(me, dense, w_gate, w_up, w_router, *blocks)


def shards(
    upstream,
    shared_down,
    shared_gate,
    shared_up,
    router_weight,
    gate_pre,
    up_pre,
    gate_grad,
    gate_scores,
    expert_ids,
):
    n = lax.axis_size("expert")
    chips = n // 2
    me = lax.axis_index("expert").astype(jnp.int32).reshape(1)
    tokens, width = upstream.shape[1:]
    rows = tokens // n
    sizes = cut(rows)
    starts = [sum(sizes[:c]) for c in range(len(sizes))]
    chunks = len(sizes)
    grads = upstream.reshape(n, rows, width)
    arrived, sent = [], []
    dense = routed_grad(gate_grad[0], gate_scores[0], expert_ids[0], router_weight.shape[2])
    for c in range(chunks):
        if c == 0:
            piece = take_rows(grads, 0, sizes[0])
            grads, dense = in_order(grads, dense)
        else:
            piece = grads[:, starts[c] : starts[c] + sizes[c]]
        if c >= IN_FLIGHT:
            piece, arrived[c - IN_FLIGHT] = in_order(piece, arrived[c - IN_FLIGHT])
        arrived.append(back_one(piece))
    dense = dense.reshape(n, rows, -1)

    def at(point, c, x):
        for p in NEED.get((point, c), ()):
            x, arrived[p] = in_order(x, arrived[p])
        for p in WAIT.get((point, c), ()):
            x, sent[p] = in_order(x, sent[p])
        return x

    def partial_sums(c):
        own, *others = first_product(me, arrived[c], shared_down[0], c > 0)
        others[0] = at("rs", c, others[0])
        return [own] + [to_expert(x, j + 1) for j, x in enumerate(others)]

    arrived[0], dense = in_order(arrived[0], dense)
    own = activation(gate_pre[0], up_pre[0], starts[0], partial_sums(0))
    for c in range(chunks):
        own = at("agy", c, own)
        near = [own] + [to_expert(own, 2 * step) for step in range(1, chips)]
        far = [to_other_core(own)]
        if c + 1 < chunks:
            arrived[c + 1], own = in_order(arrived[c + 1], own)
            partials = partial_sums(c + 1)
            partials[0], near[-1] = in_order(partials[0], near[-1])
        near[-1] = at("agc", c, near[-1])
        far += [to_other_core(x) for x in near[1:]]
        far[-1] = at("mm2", c, far[-1])
        blocks = [x for pair in zip(near, far) for x in pair]
        pieces = [sizes[c]]
        if c + 1 == chunks and sizes[c] > LAST:
            pieces = [sizes[c] - LAST, LAST]
        result, *last = second_product(
            me, blocks, starts[c], dense, shared_gate[0], shared_up[0], router_weight[0], pieces
        )
        if c + 1 < chunks:
            partials[0], result = in_order(partials[0], result)
            partials[0] = at("act", c + 1, partials[0])
            own = activation(gate_pre[0], up_pre[0], starts[c + 1], partials)
        result = at("out", c, result)
        sent.append(back_one(result))
    out = jnp.zeros((n, rows, width), jnp.bfloat16)
    for c in range(chunks - 1):
        out = lax.dynamic_update_slice(out, sent[c], (0, starts[c], 0))
    out = put_rows(out, sent[-1], starts[-1])
    for piece in last:
        out = put_rows(out, back_one(piece), rows - LAST)
    return out.reshape(1, tokens, width)


def solution(mesh):
    in_specs = (
        P("pipe", None, "expert"),
        P("pipe", None, "expert"),
        P("pipe", "expert", None),
        P("pipe", "expert", None),
        P("pipe", "expert", None),
        P("pipe", "expert", None),
        P("pipe", "expert", None),
        P("pipe", None, None),
        P("pipe", None, None),
        P("pipe", None, None),
    )
    out_specs = P("pipe", None, "expert")
    return jax.shard_map(shards, mesh=mesh, in_specs=in_specs, out_specs=out_specs, check_vma=False)
```

```python
import functools

import jax
import jax.numpy as jnp
from jax import lax
from jax.experimental import pallas as pl
from jax.experimental.pallas import tpu as pltpu
from jax.sharding import PartitionSpec as P

CHUNKS = 4
LAST = 16
IN_FLIGHT = 2
NEED = {("act", 1): (2,), ("act", 2): (3,)}
WAIT = {("act", 3): (0,), ("mm2", 3): (1,), ("out", 2): (0,), ("out", 3): (1,)}
FREE = pl.CostEstimate(flops=0, bytes_accessed=0, transcendentals=0)


def params(**kwargs):
    return pltpu.CompilerParams(vmem_limit_bytes=48 * 1024 * 1024, **kwargs)


def block_of(size, most):
    fits = [b for b in range(128, min(size, most) + 1, 128) if size % b == 0]
    return fits[-1] if fits else size


def back_one(x):
    length = lax.axis_size("pipe")
    return lax.ppermute(x, "pipe", [(i, (i - 1) % length) for i in range(length)])


def to_expert(x, by):
    n = lax.axis_size("expert")
    return lax.ppermute(x, "expert", [(i, (i + by) % n) for i in range(n)])


def to_other_core(x):
    n = lax.axis_size("expert")
    return lax.ppermute(x, "expert", [(i, i ^ 1) for i in range(n)])


def in_hbm(x):
    return pltpu.with_memory_space_constraint(x, pltpu.HBM)


def in_order(later, earlier):
    return lax.optimization_barrier((later, earlier))


def contract_last(left, right):
    return lax.dot_general(
        left, right, (((1,), (1,)), ((), ())), preferred_element_type=jnp.float32
    )


def take_kernel(start, source, target, sem):
    here = pl.ds(start, target.shape[1])
    copy = pltpu.make_async_copy(source.at[:, here], target, sem)
    copy.start()
    copy.wait()


def put_kernel(start, on, source, old, target, sem):
    del old

    def put():
        here = pl.ds(start, source.shape[1])
        copy = pltpu.make_async_copy(source, target.at[:, here], sem)
        copy.start()
        copy.wait()

    is_last = lax.axis_index("pipe") == lax.axis_size("pipe") - 1
    if on == "all":
        put()
    else:
        pl.when(is_last if on == "last" else jnp.logical_not(is_last))(put)


def take_rows(array, start, size):
    n, _, width = array.shape
    return pl.pallas_call(
        functools.partial(take_kernel, start),
        out_shape=pltpu.VMEM((n, size, width), array.dtype),
        in_specs=[pl.BlockSpec(memory_space=pltpu.HBM)],
        out_specs=pl.BlockSpec(memory_space=pltpu.VMEM),
        scratch_shapes=[pltpu.SemaphoreType.DMA],
        cost_estimate=FREE,
        name="take_rows",
    )(in_hbm(array))


def put_rows(out, piece, start, on="all"):
    return pl.pallas_call(
        functools.partial(put_kernel, start, on),
        out_shape=jax.ShapeDtypeStruct(out.shape, out.dtype),
        in_specs=[pl.BlockSpec(memory_space=pltpu.VMEM), pl.BlockSpec(memory_space=pltpu.HBM)],
        out_specs=pl.BlockSpec(memory_space=pltpu.HBM),
        scratch_shapes=[pltpu.SemaphoreType.DMA],
        input_output_aliases={1: 0},
        cost_estimate=FREE,
        name="put_rows",
    )(pltpu.with_memory_space_constraint(piece, pltpu.VMEM), out)


def routed_kernel(grad_ref, score_ref, chosen_ref, out_ref):
    grad, scores, chosen = grad_ref[...], score_ref[...], chosen_ref[...]
    total = jnp.sum(scores, axis=0, keepdims=True)
    mixed = jnp.sum(grad * scores, axis=0, keepdims=True)
    logit_grad = 2.5 * (grad - mixed / total) / total * scores * (1.0 - scores)
    experts = lax.broadcasted_iota(jnp.int32, out_ref.shape[::-1], 0)
    dense = jnp.zeros(experts.shape, jnp.float32)
    for slot in range(grad.shape[0]):
        here = chosen[slot : slot + 1] == experts
        dense = dense + jnp.where(here, logit_grad[slot : slot + 1], 0.0)
    out_ref[...] = dense.T.astype(out_ref.dtype)


def routed_grad(grad, scores, chosen, n_experts):
    tokens, top = grad.shape
    block = block_of(tokens, 128)
    spec = pl.BlockSpec((top, block), lambda i: (0, i))
    return pl.pallas_call(
        routed_kernel,
        out_shape=jax.ShapeDtypeStruct((tokens, n_experts), jnp.bfloat16),
        grid=(tokens // block,),
        in_specs=[spec, spec, spec],
        out_specs=pl.BlockSpec((block, n_experts), lambda i: (i, 0)),
        cost_estimate=FREE,
        name="routed_grad",
    )(in_hbm(grad.T), in_hbm(scores.T), in_hbm(chosen.T))


def first_kernel(n, me_ref, rows_ref, weight_ref, *out_refs):
    me = me_ref[0]
    part = rows_ref.shape[1]
    left = jnp.concatenate([rows_ref[lax.rem(me + j, n)] for j in range(n)], axis=0)
    product = contract_last(left, weight_ref[...]).astype(jnp.bfloat16)
    for j in range(n):
        out_refs[j][...] = product[j * part : (j + 1) * part]


def first_product(me, rows, weight, late):
    n, part, width = rows.shape
    hidden = weight.shape[0]
    block = block_of(hidden, 256)
    return pl.pallas_call(
        functools.partial(first_kernel, n),
        out_shape=[jax.ShapeDtypeStruct((part, hidden), jnp.bfloat16)] * n,
        grid_spec=pltpu.PrefetchScalarGridSpec(
            num_scalar_prefetch=1,
            grid=(hidden // block,),
            in_specs=[
                pl.BlockSpec((n, part, width), lambda i, me: (0, 0, 0)),
                pl.BlockSpec((block, width), lambda i, me: (i, 0)),
            ],
            out_specs=[pl.BlockSpec((part, block), lambda i, me: (0, i))] * n,
        ),
        compiler_params=params(),
        cost_estimate=FREE,
        name="first_product",
    )(me, rows, weight if late else in_hbm(weight))


def activation_kernel(gate_ref, up_ref, *refs):
    *part_refs, out_ref = refs
    hidden = gate_ref.shape[1]
    hidden_grad = part_refs[0][...].astype(jnp.float32)
    for ref in part_refs[1:]:
        hidden_grad = hidden_grad + ref[...].astype(jnp.float32)
    act_a = gate_ref[...].astype(jnp.float32)
    act_b = up_ref[...].astype(jnp.float32)
    sigma = 1.0 / (1.0 + jnp.exp(-act_a))
    gate_part = hidden_grad * act_b * sigma * (1.0 + act_a * (1.0 - sigma))
    up_part = hidden_grad * act_a * sigma
    out_ref[:, :hidden] = gate_part.astype(out_ref.dtype)
    out_ref[:, hidden:] = up_part.astype(out_ref.dtype)


def activation(gate_pre, up_pre, c, partials):
    part, hidden = partials[0].shape
    saved = pl.BlockSpec((part, hidden), lambda i: (c, 0))
    return pl.pallas_call(
        activation_kernel,
        out_shape=jax.ShapeDtypeStruct((part, 2 * hidden), jnp.bfloat16),
        grid=(1,),
        in_specs=[saved, saved] + [pl.BlockSpec((part, hidden), lambda i: (0, 0))] * len(partials),
        out_specs=pl.BlockSpec((part, 2 * hidden), lambda i: (0, 0)),
        compiler_params=params(),
        cost_estimate=FREE,
        name="activation",
    )(in_hbm(gate_pre), in_hbm(up_pre), *partials)


def second_kernel(n, me_ref, dense_ref, gate_ref, up_ref, router_ref, *refs):
    block_refs, out_refs, held = refs[:n], refs[n:-1], refs[-1]
    chips = n // 2
    hidden = gate_ref.shape[1]

    @pl.when(pl.program_id(0) == 0)
    def _():
        me = me_ref[0]
        chip, core = me // 2, lax.rem(me, 2)
        for step in range(chips):
            there = lax.rem(chip - step + chips, chips) * 2
            held[there + core] = block_refs[2 * step][...]
            held[there + 1 - core] = block_refs[2 * step + 1][...]

    both = held[...].reshape(-1, 2 * hidden)
    result = contract_last(both[:, :hidden], gate_ref[...])
    result = result + contract_last(both[:, hidden:], up_ref[...])
    dense = dense_ref[...].reshape(both.shape[0], -1)
    result = result + contract_last(dense, router_ref[...])
    result = result.astype(jnp.bfloat16).reshape(n, held.shape[1], -1)
    first = 0
    for out_ref in out_refs:
        size = out_ref.shape[1]
        out_ref[...] = result[:, first : first + size]
        first += size


def second_product(me, blocks, c, dense, w_gate, w_up, w_router, sizes):
    n = len(blocks)
    part, both = blocks[0].shape
    width, hidden = w_gate.shape
    n_experts = w_router.shape[1]
    block = block_of(width, 256)
    return pl.pallas_call(
        functools.partial(second_kernel, n),
        out_shape=[jax.ShapeDtypeStruct((n, size, width), jnp.bfloat16) for size in sizes],
        grid_spec=pltpu.PrefetchScalarGridSpec(
            num_scalar_prefetch=1,
            grid=(width // block,),
            in_specs=[
                pl.BlockSpec((n, part, n_experts), lambda i, me: (0, c, 0)),
                pl.BlockSpec((block, hidden), lambda i, me: (i, 0)),
                pl.BlockSpec((block, hidden), lambda i, me: (i, 0)),
                pl.BlockSpec((block, n_experts), lambda i, me: (i, 0)),
            ]
            + [pl.BlockSpec((part, both), lambda i, me: (0, 0))] * n,
            out_specs=[pl.BlockSpec((n, size, block), lambda i, me: (0, 0, i)) for size in sizes],
            scratch_shapes=[pltpu.VMEM((n, part, both), jnp.bfloat16)],
        ),
        compiler_params=params(),
        cost_estimate=FREE,
        name="second_product",
    )(me, dense, w_gate, w_up, w_router, *blocks)


def shards(
    upstream,
    shared_down,
    shared_gate,
    shared_up,
    router_weight,
    gate_pre,
    up_pre,
    gate_grad,
    gate_scores,
    expert_ids,
):
    n = lax.axis_size("expert")
    chips = n // 2
    me = lax.axis_index("expert").astype(jnp.int32).reshape(1)
    tokens, width = upstream.shape[1:]
    rows = tokens // n
    chunks = min(CHUNKS, rows // 16)
    part = rows // chunks
    grads = upstream.reshape(n, rows, width)
    arrived, sent = [], []
    dense = routed_grad(gate_grad[0], gate_scores[0], expert_ids[0], router_weight.shape[2])
    for c in range(chunks):
        if c == 0:
            piece = take_rows(grads, 0, part)
            grads, dense = in_order(grads, dense)
        else:
            piece = grads[:, c * part : (c + 1) * part]
        if c >= IN_FLIGHT:
            piece, arrived[c - IN_FLIGHT] = in_order(piece, arrived[c - IN_FLIGHT])
        arrived.append(back_one(piece))
    dense = dense.reshape(n, rows, -1)

    def at(point, c, x):
        for p in NEED.get((point, c), ()):
            x, arrived[p] = in_order(x, arrived[p])
        for p in WAIT.get((point, c), ()):
            x, sent[p] = in_order(x, sent[p])
        return x

    def partial_sums(c):
        own, *others = first_product(me, arrived[c], shared_down[0], c > 0)
        others[0] = at("rs", c, others[0])
        return [own] + [to_expert(x, j + 1) for j, x in enumerate(others)]

    arrived[0], dense = in_order(arrived[0], dense)
    own = activation(gate_pre[0], up_pre[0], 0, partial_sums(0))
    for c in range(chunks):
        own = at("agy", c, own)
        near = [own] + [to_expert(own, 2 * step) for step in range(1, chips)]
        far = [to_other_core(own)]
        if c + 1 < chunks:
            arrived[c + 1], own = in_order(arrived[c + 1], own)
            partials = partial_sums(c + 1)
            partials[0], near[-1] = in_order(partials[0], near[-1])
        near[-1] = at("agc", c, near[-1])
        far += [to_other_core(x) for x in near[1:]]
        far[-1] = at("mm2", c, far[-1])
        blocks = [x for pair in zip(near, far) for x in pair]
        sizes = [part]
        if c + 1 == chunks and part > LAST:
            sizes = [part - LAST, LAST]
        result, *last = second_product(
            me, blocks, c, dense, shared_gate[0], shared_up[0], router_weight[0], sizes
        )
        if c + 1 < chunks:
            partials[0], result = in_order(partials[0], result)
            partials[0] = at("act", c + 1, partials[0])
            own = activation(gate_pre[0], up_pre[0], c + 1, partials)
        result = at("out", c, result)
        sent.append(back_one(result))
    out = jnp.zeros((n, rows, width), jnp.bfloat16)
    for c in range(chunks - 1):
        out = lax.dynamic_update_slice(out, sent[c], (0, c * part, 0))
    out = put_rows(out, sent[-1], (chunks - 1) * part)
    length = lax.axis_size("pipe")
    for piece in last:
        near = lax.ppermute(piece, "pipe", [(i, i - 1) for i in range(1, length)])
        far = lax.ppermute(piece, "pipe", [(0, length - 1)])
        out = put_rows(out, near, rows - LAST, "others")
        out = put_rows(out, far, rows - LAST, "last")
    return out.reshape(1, tokens, width)


def solution(mesh):
    in_specs = (
        P("pipe", None, "expert"),
        P("pipe", None, "expert"),
        P("pipe", "expert", None),
        P("pipe", "expert", None),
        P("pipe", "expert", None),
        P("pipe", "expert", None),
        P("pipe", "expert", None),
        P("pipe", None, None),
        P("pipe", None, None),
        P("pipe", None, None),
    )
    out_specs = P("pipe", None, "expert")
    return jax.shard_map(shards, mesh=mesh, in_specs=in_specs, out_specs=out_specs, check_vma=False)
```

```python
import functools

import jax
import jax.numpy as jnp
from jax import lax
from jax.experimental import pallas as pl
from jax.experimental.pallas import tpu as pltpu
from jax.sharding import PartitionSpec as P

PARTS = (3, 5, 4, 4)
LAST = 16
IN_FLIGHT = 2
NEED = {("act", 1): (2,), ("act", 2): (3,)}
WAIT = {("act", 3): (0,), ("mm2", 3): (1,), ("out", 2): (0,), ("out", 3): (1,)}
FREE = pl.CostEstimate(flops=0, bytes_accessed=0, transcendentals=0)


def params(**kwargs):
    return pltpu.CompilerParams(vmem_limit_bytes=48 * 1024 * 1024, **kwargs)


def cut(rows):
    if rows % 256 == 0:
        return [rows // 16 * share for share in PARTS]
    return [rows // 4] * 4 if rows % 64 == 0 else [rows]


def block_of(size, most):
    fits = [b for b in range(128, min(size, most) + 1, 128) if size % b == 0]
    return fits[-1] if fits else size


def back_one(x):
    length = lax.axis_size("pipe")
    return lax.ppermute(x, "pipe", [(i, (i - 1) % length) for i in range(length)])


def to_expert(x, by):
    n = lax.axis_size("expert")
    return lax.ppermute(x, "expert", [(i, (i + by) % n) for i in range(n)])


def to_other_core(x):
    n = lax.axis_size("expert")
    return lax.ppermute(x, "expert", [(i, i ^ 1) for i in range(n)])


def in_hbm(x):
    return pltpu.with_memory_space_constraint(x, pltpu.HBM)


def in_order(later, earlier):
    return lax.optimization_barrier((later, earlier))


def contract_last(left, right):
    return lax.dot_general(
        left, right, (((1,), (1,)), ((), ())), preferred_element_type=jnp.float32
    )


def take_kernel(start, source, target, sem):
    here = pl.ds(start, target.shape[1])
    copy = pltpu.make_async_copy(source.at[:, here], target, sem)
    copy.start()
    copy.wait()


def put_kernel(start, on, source, old, target, sem):
    del old

    def put():
        here = pl.ds(start, source.shape[1])
        copy = pltpu.make_async_copy(source, target.at[:, here], sem)
        copy.start()
        copy.wait()

    is_last = lax.axis_index("pipe") == lax.axis_size("pipe") - 1
    if on == "all":
        put()
    else:
        pl.when(is_last if on == "last" else jnp.logical_not(is_last))(put)


def take_rows(array, start, size):
    n, _, width = array.shape
    return pl.pallas_call(
        functools.partial(take_kernel, start),
        out_shape=pltpu.VMEM((n, size, width), array.dtype),
        in_specs=[pl.BlockSpec(memory_space=pltpu.HBM)],
        out_specs=pl.BlockSpec(memory_space=pltpu.VMEM),
        scratch_shapes=[pltpu.SemaphoreType.DMA],
        cost_estimate=FREE,
        name="take_rows",
    )(in_hbm(array))


def put_rows(out, piece, start, on="all"):
    return pl.pallas_call(
        functools.partial(put_kernel, start, on),
        out_shape=jax.ShapeDtypeStruct(out.shape, out.dtype),
        in_specs=[pl.BlockSpec(memory_space=pltpu.VMEM), pl.BlockSpec(memory_space=pltpu.HBM)],
        out_specs=pl.BlockSpec(memory_space=pltpu.HBM),
        scratch_shapes=[pltpu.SemaphoreType.DMA],
        input_output_aliases={1: 0},
        cost_estimate=FREE,
        name="put_rows",
    )(pltpu.with_memory_space_constraint(piece, pltpu.VMEM), out)


def routed_kernel(grad_ref, score_ref, chosen_ref, out_ref):
    grad, scores, chosen = grad_ref[...], score_ref[...], chosen_ref[...]
    total = jnp.sum(scores, axis=0, keepdims=True)
    mixed = jnp.sum(grad * scores, axis=0, keepdims=True)
    logit_grad = 2.5 * (grad - mixed / total) / total * scores * (1.0 - scores)
    experts = lax.broadcasted_iota(jnp.int32, out_ref.shape[::-1], 0)
    dense = jnp.zeros(experts.shape, jnp.float32)
    for slot in range(grad.shape[0]):
        here = chosen[slot : slot + 1] == experts
        dense = dense + jnp.where(here, logit_grad[slot : slot + 1], 0.0)
    out_ref[...] = dense.T.astype(out_ref.dtype)


def routed_grad(grad, scores, chosen, n_experts):
    tokens, top = grad.shape
    block = block_of(tokens, 128)
    spec = pl.BlockSpec((top, block), lambda i: (0, i))
    return pl.pallas_call(
        routed_kernel,
        out_shape=jax.ShapeDtypeStruct((tokens, n_experts), jnp.bfloat16),
        grid=(tokens // block,),
        in_specs=[spec, spec, spec],
        out_specs=pl.BlockSpec((block, n_experts), lambda i: (i, 0)),
        cost_estimate=FREE,
        name="routed_grad",
    )(in_hbm(grad.T), in_hbm(scores.T), in_hbm(chosen.T))


def first_kernel(n, me_ref, rows_ref, weight_ref, *out_refs):
    me = me_ref[0]
    part = rows_ref.shape[1]
    left = jnp.concatenate([rows_ref[lax.rem(me + j, n)] for j in range(n)], axis=0)
    product = contract_last(left, weight_ref[...]).astype(jnp.bfloat16)
    for j in range(n):
        out_refs[j][...] = product[j * part : (j + 1) * part]


def first_product(me, rows, weight, late):
    n, part, width = rows.shape
    hidden = weight.shape[0]
    block = block_of(hidden, 256)
    return pl.pallas_call(
        functools.partial(first_kernel, n),
        out_shape=[jax.ShapeDtypeStruct((part, hidden), jnp.bfloat16)] * n,
        grid_spec=pltpu.PrefetchScalarGridSpec(
            num_scalar_prefetch=1,
            grid=(hidden // block,),
            in_specs=[
                pl.BlockSpec((n, part, width), lambda i, me: (0, 0, 0)),
                pl.BlockSpec((block, width), lambda i, me: (i, 0)),
            ],
            out_specs=[pl.BlockSpec((part, block), lambda i, me: (0, i))] * n,
        ),
        compiler_params=params(),
        cost_estimate=FREE,
        name="first_product",
    )(me, rows, weight if late else in_hbm(weight))


def activation_kernel(start, gate_ref, up_ref, *refs):
    *part_refs, out_ref = refs
    part, hidden = part_refs[0].shape
    here = slice(start, start + part)
    hidden_grad = part_refs[0][...].astype(jnp.float32)
    for ref in part_refs[1:]:
        hidden_grad = hidden_grad + ref[...].astype(jnp.float32)
    act_a = gate_ref[here].astype(jnp.float32)
    act_b = up_ref[here].astype(jnp.float32)
    sigma = 1.0 / (1.0 + jnp.exp(-act_a))
    gate_part = hidden_grad * act_b * sigma * (1.0 + act_a * (1.0 - sigma))
    up_part = hidden_grad * act_a * sigma
    out_ref[:, :hidden] = gate_part.astype(out_ref.dtype)
    out_ref[:, hidden:] = up_part.astype(out_ref.dtype)


def activation(gate_pre, up_pre, start, partials):
    part, hidden = partials[0].shape
    saved = pl.BlockSpec(gate_pre.shape, lambda i: (0, 0))
    return pl.pallas_call(
        functools.partial(activation_kernel, start),
        out_shape=jax.ShapeDtypeStruct((part, 2 * hidden), jnp.bfloat16),
        grid=(1,),
        in_specs=[saved, saved] + [pl.BlockSpec((part, hidden), lambda i: (0, 0))] * len(partials),
        out_specs=pl.BlockSpec((part, 2 * hidden), lambda i: (0, 0)),
        compiler_params=params(),
        cost_estimate=FREE,
        name="activation",
    )(in_hbm(gate_pre), in_hbm(up_pre), *partials)


def second_kernel(n, start, me_ref, dense_ref, gate_ref, up_ref, router_ref, *refs):
    block_refs, out_refs, held = refs[:n], refs[n:-1], refs[-1]
    chips = n // 2
    hidden = gate_ref.shape[1]

    @pl.when(pl.program_id(0) == 0)
    def _():
        me = me_ref[0]
        chip, core = me // 2, lax.rem(me, 2)
        for step in range(chips):
            there = lax.rem(chip - step + chips, chips) * 2
            held[there + core] = block_refs[2 * step][...]
            held[there + 1 - core] = block_refs[2 * step + 1][...]

    both = held[...].reshape(-1, 2 * hidden)
    result = contract_last(both[:, :hidden], gate_ref[...])
    result = result + contract_last(both[:, hidden:], up_ref[...])
    dense = dense_ref[:, start : start + held.shape[1]].reshape(both.shape[0], -1)
    result = result + contract_last(dense, router_ref[...])
    result = result.astype(jnp.bfloat16).reshape(n, held.shape[1], -1)
    first = 0
    for out_ref in out_refs:
        size = out_ref.shape[1]
        out_ref[...] = result[:, first : first + size]
        first += size


def second_product(me, blocks, start, dense, w_gate, w_up, w_router, sizes):
    n = len(blocks)
    part, both = blocks[0].shape
    width, hidden = w_gate.shape
    n_experts = w_router.shape[1]
    block = block_of(width, 256)
    return pl.pallas_call(
        functools.partial(second_kernel, n, start),
        out_shape=[jax.ShapeDtypeStruct((n, size, width), jnp.bfloat16) for size in sizes],
        grid_spec=pltpu.PrefetchScalarGridSpec(
            num_scalar_prefetch=1,
            grid=(width // block,),
            in_specs=[
                pl.BlockSpec(dense.shape, lambda i, me: (0, 0, 0)),
                pl.BlockSpec((block, hidden), lambda i, me: (i, 0)),
                pl.BlockSpec((block, hidden), lambda i, me: (i, 0)),
                pl.BlockSpec((block, n_experts), lambda i, me: (i, 0)),
            ]
            + [pl.BlockSpec((part, both), lambda i, me: (0, 0))] * n,
            out_specs=[pl.BlockSpec((n, size, block), lambda i, me: (0, 0, i)) for size in sizes],
            scratch_shapes=[pltpu.VMEM((n, part, both), jnp.bfloat16)],
        ),
        compiler_params=params(),
        cost_estimate=FREE,
        name="second_product",
    )(me, dense, w_gate, w_up, w_router, *blocks)


def shards(
    upstream,
    shared_down,
    shared_gate,
    shared_up,
    router_weight,
    gate_pre,
    up_pre,
    gate_grad,
    gate_scores,
    expert_ids,
):
    n = lax.axis_size("expert")
    chips = n // 2
    me = lax.axis_index("expert").astype(jnp.int32).reshape(1)
    tokens, width = upstream.shape[1:]
    rows = tokens // n
    sizes = cut(rows)
    starts = [sum(sizes[:c]) for c in range(len(sizes))]
    chunks = len(sizes)
    grads = upstream.reshape(n, rows, width)
    arrived, sent = [], []
    dense = routed_grad(gate_grad[0], gate_scores[0], expert_ids[0], router_weight.shape[2])
    for c in range(chunks):
        if c == 0:
            piece = take_rows(grads, 0, sizes[0])
            grads, dense = in_order(grads, dense)
        else:
            piece = grads[:, starts[c] : starts[c] + sizes[c]]
        if c >= IN_FLIGHT:
            piece, arrived[c - IN_FLIGHT] = in_order(piece, arrived[c - IN_FLIGHT])
        arrived.append(back_one(piece))
    dense = dense.reshape(n, rows, -1)

    def at(point, c, x):
        for p in NEED.get((point, c), ()):
            x, arrived[p] = in_order(x, arrived[p])
        for p in WAIT.get((point, c), ()):
            x, sent[p] = in_order(x, sent[p])
        return x

    def partial_sums(c):
        own, *others = first_product(me, arrived[c], shared_down[0], c > 0)
        others[0] = at("rs", c, others[0])
        return [own] + [to_expert(x, j + 1) for j, x in enumerate(others)]

    arrived[0], dense = in_order(arrived[0], dense)
    own = activation(gate_pre[0], up_pre[0], starts[0], partial_sums(0))
    for c in range(chunks):
        own = at("agy", c, own)
        near = [own] + [to_expert(own, 2 * step) for step in range(1, chips)]
        far = [to_other_core(own)]
        if c + 1 < chunks:
            arrived[c + 1], own = in_order(arrived[c + 1], own)
            partials = partial_sums(c + 1)
            partials[0], near[-1] = in_order(partials[0], near[-1])
        near[-1] = at("agc", c, near[-1])
        far += [to_other_core(x) for x in near[1:]]
        far[-1] = at("mm2", c, far[-1])
        blocks = [x for pair in zip(near, far) for x in pair]
        pieces = [sizes[c]]
        if c + 1 == chunks and sizes[c] > LAST:
            pieces = [sizes[c] - LAST, LAST]
        result, *last = second_product(
            me, blocks, starts[c], dense, shared_gate[0], shared_up[0], router_weight[0], pieces
        )
        if c + 1 < chunks:
            partials[0], result = in_order(partials[0], result)
            partials[0] = at("act", c + 1, partials[0])
            own = activation(gate_pre[0], up_pre[0], starts[c + 1], partials)
        result = at("out", c, result)
        sent.append(back_one(result))
    out = jnp.zeros((n, rows, width), jnp.bfloat16)
    for c in range(chunks - 1):
        out = lax.dynamic_update_slice(out, sent[c], (0, starts[c], 0))
    out = put_rows(out, sent[-1], starts[-1])
    length = lax.axis_size("pipe")
    for piece in last:
        near = lax.ppermute(piece, "pipe", [(i, i - 1) for i in range(1, length)])
        far = lax.ppermute(piece, "pipe", [(0, length - 1)])
        out = put_rows(out, near, rows - LAST, "others")
        out = put_rows(out, far, rows - LAST, "last")
    return out.reshape(1, tokens, width)


def solution(mesh):
    in_specs = (
        P("pipe", None, "expert"),
        P("pipe", None, "expert"),
        P("pipe", "expert", None),
        P("pipe", "expert", None),
        P("pipe", "expert", None),
        P("pipe", "expert", None),
        P("pipe", "expert", None),
        P("pipe", None, None),
        P("pipe", None, None),
        P("pipe", None, None),
    )
    out_specs = P("pipe", None, "expert")
    return jax.shard_map(shards, mesh=mesh, in_specs=in_specs, out_specs=out_specs, check_vma=False)
```

```python
import functools

import jax
import jax.numpy as jnp
from jax import lax
from jax.experimental import pallas as pl
from jax.experimental.pallas import tpu as pltpu
from jax.sharding import PartitionSpec as P

PARTS = (3, 5, 4, 4)
LAST = 16
IN_FLIGHT = 2
NEED = {("act", 1): (2,), ("act", 2): (3,)}
WAIT = {("act", 3): (0,), ("mm2", 3): (1,), ("out", 2): (0,), ("out", 3): (1,)}
FREE = pl.CostEstimate(flops=0, bytes_accessed=0, transcendentals=0)


def params(**kwargs):
    return pltpu.CompilerParams(vmem_limit_bytes=48 * 1024 * 1024, **kwargs)


def cut(rows):
    if rows % 256 == 0:
        return [rows // 16 * share for share in PARTS]
    return [rows // 4] * 4 if rows % 64 == 0 else [rows]


def block_of(size, most):
    fits = [b for b in range(128, min(size, most) + 1, 128) if size % b == 0]
    return fits[-1] if fits else size


def back_one(x):
    length = lax.axis_size("pipe")
    return lax.ppermute(x, "pipe", [(i, (i - 1) % length) for i in range(length)])


def to_expert(x, by):
    n = lax.axis_size("expert")
    return lax.ppermute(x, "expert", [(i, (i + by) % n) for i in range(n)])


def to_other_core(x):
    n = lax.axis_size("expert")
    return lax.ppermute(x, "expert", [(i, i ^ 1) for i in range(n)])


def in_hbm(x):
    return pltpu.with_memory_space_constraint(x, pltpu.HBM)


def in_order(later, earlier):
    return lax.optimization_barrier((later, earlier))


def contract_last(left, right):
    return lax.dot_general(
        left, right, (((1,), (1,)), ((), ())), preferred_element_type=jnp.float32
    )


def take_kernel(start, source, target, sems):
    here = pl.ds(start, target.shape[1])
    half = target.shape[0] // 2
    copies = [
        pltpu.make_async_copy(
            source.at[pl.ds(i * half, half), here], target.at[pl.ds(i * half, half)], sems.at[i]
        )
        for i in range(2)
    ]
    for copy in copies:
        copy.start()
    for copy in copies:
        copy.wait()


def put_kernel(start, on, source, old, target, sem):
    del old

    def put():
        here = pl.ds(start, source.shape[1])
        copy = pltpu.make_async_copy(source, target.at[:, here], sem)
        copy.start()
        copy.wait()

    is_last = lax.axis_index("pipe") == lax.axis_size("pipe") - 1
    if on == "all":
        put()
    else:
        pl.when(is_last if on == "last" else jnp.logical_not(is_last))(put)


def take_rows(array, start, size):
    n, _, width = array.shape
    return pl.pallas_call(
        functools.partial(take_kernel, start),
        out_shape=pltpu.VMEM((n, size, width), array.dtype),
        in_specs=[pl.BlockSpec(memory_space=pltpu.HBM)],
        out_specs=pl.BlockSpec(memory_space=pltpu.VMEM),
        scratch_shapes=[pltpu.SemaphoreType.DMA((2,))],
        cost_estimate=FREE,
        name="take_rows",
    )(in_hbm(array))


def put_rows(out, piece, start, on="all"):
    return pl.pallas_call(
        functools.partial(put_kernel, start, on),
        out_shape=jax.ShapeDtypeStruct(out.shape, out.dtype),
        in_specs=[pl.BlockSpec(memory_space=pltpu.VMEM), pl.BlockSpec(memory_space=pltpu.HBM)],
        out_specs=pl.BlockSpec(memory_space=pltpu.HBM),
        scratch_shapes=[pltpu.SemaphoreType.DMA],
        input_output_aliases={1: 0},
        cost_estimate=FREE,
        name="put_rows",
    )(pltpu.with_memory_space_constraint(piece, pltpu.VMEM), out)


def routed_kernel(grad_ref, score_ref, chosen_ref, out_ref):
    grad, scores, chosen = grad_ref[...], score_ref[...], chosen_ref[...]
    total = jnp.sum(scores, axis=0, keepdims=True)
    mixed = jnp.sum(grad * scores, axis=0, keepdims=True)
    logit_grad = 2.5 * (grad - mixed / total) / total * scores * (1.0 - scores)
    experts = lax.broadcasted_iota(jnp.int32, out_ref.shape[::-1], 0)
    dense = jnp.zeros(experts.shape, jnp.float32)
    for slot in range(grad.shape[0]):
        here = chosen[slot : slot + 1] == experts
        dense = dense + jnp.where(here, logit_grad[slot : slot + 1], 0.0)
    out_ref[...] = dense.T.astype(out_ref.dtype)


def routed_grad(grad, scores, chosen, n_experts):
    tokens, top = grad.shape
    block = block_of(tokens, 128)
    spec = pl.BlockSpec((top, block), lambda i: (0, i))
    return pl.pallas_call(
        routed_kernel,
        out_shape=jax.ShapeDtypeStruct((tokens, n_experts), jnp.bfloat16),
        grid=(tokens // block,),
        in_specs=[spec, spec, spec],
        out_specs=pl.BlockSpec((block, n_experts), lambda i: (i, 0)),
        cost_estimate=FREE,
        name="routed_grad",
    )(in_hbm(grad.T), in_hbm(scores.T), in_hbm(chosen.T))


def first_kernel(n, me_ref, rows_ref, weight_ref, *out_refs):
    me = me_ref[0]
    part = rows_ref.shape[1]
    left = jnp.concatenate([rows_ref[lax.rem(me + j, n)] for j in range(n)], axis=0)
    product = contract_last(left, weight_ref[...]).astype(jnp.bfloat16)
    for j in range(n):
        out_refs[j][...] = product[j * part : (j + 1) * part]


def first_product(me, rows, weight, late):
    n, part, width = rows.shape
    hidden = weight.shape[0]
    block = block_of(hidden, 256)
    return pl.pallas_call(
        functools.partial(first_kernel, n),
        out_shape=[jax.ShapeDtypeStruct((part, hidden), jnp.bfloat16)] * n,
        grid_spec=pltpu.PrefetchScalarGridSpec(
            num_scalar_prefetch=1,
            grid=(hidden // block,),
            in_specs=[
                pl.BlockSpec((n, part, width), lambda i, me: (0, 0, 0)),
                pl.BlockSpec((block, width), lambda i, me: (i, 0)),
            ],
            out_specs=[pl.BlockSpec((part, block), lambda i, me: (0, i))] * n,
        ),
        compiler_params=params(),
        cost_estimate=FREE,
        name="first_product",
    )(me, rows, weight if late else in_hbm(weight))


def activation_kernel(start, gate_ref, up_ref, *refs):
    *part_refs, out_ref = refs
    part, hidden = part_refs[0].shape
    here = slice(start, start + part)
    hidden_grad = part_refs[0][...].astype(jnp.float32)
    for ref in part_refs[1:]:
        hidden_grad = hidden_grad + ref[...].astype(jnp.float32)
    act_a = gate_ref[here].astype(jnp.float32)
    act_b = up_ref[here].astype(jnp.float32)
    sigma = 1.0 / (1.0 + jnp.exp(-act_a))
    gate_part = hidden_grad * act_b * sigma * (1.0 + act_a * (1.0 - sigma))
    up_part = hidden_grad * act_a * sigma
    out_ref[:, :hidden] = gate_part.astype(out_ref.dtype)
    out_ref[:, hidden:] = up_part.astype(out_ref.dtype)


def activation(gate_pre, up_pre, start, partials):
    part, hidden = partials[0].shape
    saved = pl.BlockSpec(gate_pre.shape, lambda i: (0, 0))
    return pl.pallas_call(
        functools.partial(activation_kernel, start),
        out_shape=jax.ShapeDtypeStruct((part, 2 * hidden), jnp.bfloat16),
        grid=(1,),
        in_specs=[saved, saved] + [pl.BlockSpec((part, hidden), lambda i: (0, 0))] * len(partials),
        out_specs=pl.BlockSpec((part, 2 * hidden), lambda i: (0, 0)),
        compiler_params=params(),
        cost_estimate=FREE,
        name="activation",
    )(in_hbm(gate_pre), in_hbm(up_pre), *partials)


def second_kernel(n, start, me_ref, dense_ref, gate_ref, up_ref, router_ref, *refs):
    block_refs, out_refs, held = refs[:n], refs[n:-1], refs[-1]
    chips = n // 2
    hidden = gate_ref.shape[1]

    @pl.when(pl.program_id(0) == 0)
    def _():
        me = me_ref[0]
        chip, core = me // 2, lax.rem(me, 2)
        for step in range(chips):
            there = lax.rem(chip - step + chips, chips) * 2
            held[there + core] = block_refs[2 * step][...]
            held[there + 1 - core] = block_refs[2 * step + 1][...]

    both = held[...].reshape(-1, 2 * hidden)
    result = contract_last(both[:, :hidden], gate_ref[...])
    result = result + contract_last(both[:, hidden:], up_ref[...])
    dense = dense_ref[:, start : start + held.shape[1]].reshape(both.shape[0], -1)
    result = result + contract_last(dense, router_ref[...])
    result = result.astype(jnp.bfloat16).reshape(n, held.shape[1], -1)
    first = 0
    for out_ref in out_refs:
        size = out_ref.shape[1]
        out_ref[...] = result[:, first : first + size]
        first += size


def second_product(me, blocks, start, dense, w_gate, w_up, w_router, sizes):
    n = len(blocks)
    part, both = blocks[0].shape
    width, hidden = w_gate.shape
    n_experts = w_router.shape[1]
    block = block_of(width, 256)
    return pl.pallas_call(
        functools.partial(second_kernel, n, start),
        out_shape=[jax.ShapeDtypeStruct((n, size, width), jnp.bfloat16) for size in sizes],
        grid_spec=pltpu.PrefetchScalarGridSpec(
            num_scalar_prefetch=1,
            grid=(width // block,),
            in_specs=[
                pl.BlockSpec(dense.shape, lambda i, me: (0, 0, 0)),
                pl.BlockSpec((block, hidden), lambda i, me: (i, 0)),
                pl.BlockSpec((block, hidden), lambda i, me: (i, 0)),
                pl.BlockSpec((block, n_experts), lambda i, me: (i, 0)),
            ]
            + [pl.BlockSpec((part, both), lambda i, me: (0, 0))] * n,
            out_specs=[pl.BlockSpec((n, size, block), lambda i, me: (0, 0, i)) for size in sizes],
            scratch_shapes=[pltpu.VMEM((n, part, both), jnp.bfloat16)],
        ),
        compiler_params=params(),
        cost_estimate=FREE,
        name="second_product",
    )(me, dense, w_gate, w_up, w_router, *blocks)


def shards(
    upstream,
    shared_down,
    shared_gate,
    shared_up,
    router_weight,
    gate_pre,
    up_pre,
    gate_grad,
    gate_scores,
    expert_ids,
):
    n = lax.axis_size("expert")
    chips = n // 2
    me = lax.axis_index("expert").astype(jnp.int32).reshape(1)
    tokens, width = upstream.shape[1:]
    rows = tokens // n
    sizes = cut(rows)
    starts = [sum(sizes[:c]) for c in range(len(sizes))]
    chunks = len(sizes)
    grads = upstream.reshape(n, rows, width)
    arrived, sent = [], []
    dense = routed_grad(gate_grad[0], gate_scores[0], expert_ids[0], router_weight.shape[2])
    for c in range(chunks):
        if c == 0:
            piece = take_rows(grads, 0, sizes[0])
            grads, dense = in_order(grads, dense)
        else:
            piece = grads[:, starts[c] : starts[c] + sizes[c]]
        if c >= IN_FLIGHT:
            piece, arrived[c - IN_FLIGHT] = in_order(piece, arrived[c - IN_FLIGHT])
        arrived.append(back_one(piece))
    dense = dense.reshape(n, rows, -1)

    def at(point, c, x):
        for p in NEED.get((point, c), ()):
            x, arrived[p] = in_order(x, arrived[p])
        for p in WAIT.get((point, c), ()):
            x, sent[p] = in_order(x, sent[p])
        return x

    def partial_sums(c):
        own, *others = first_product(me, arrived[c], shared_down[0], c > 0)
        others[0] = at("rs", c, others[0])
        return [own] + [to_expert(x, j + 1) for j, x in enumerate(others)]

    arrived[0], dense = in_order(arrived[0], dense)
    own = activation(gate_pre[0], up_pre[0], starts[0], partial_sums(0))
    for c in range(chunks):
        own = at("agy", c, own)
        near = [own] + [to_expert(own, 2 * step) for step in range(1, chips)]
        far = [to_other_core(own)]
        if c + 1 < chunks:
            arrived[c + 1], own = in_order(arrived[c + 1], own)
            partials = partial_sums(c + 1)
            partials[0], near[-1] = in_order(partials[0], near[-1])
        near[-1] = at("agc", c, near[-1])
        far += [to_other_core(x) for x in near[1:]]
        far[-1] = at("mm2", c, far[-1])
        blocks = [x for pair in zip(near, far) for x in pair]
        pieces = [sizes[c]]
        if c + 1 == chunks and sizes[c] > LAST:
            pieces = [sizes[c] - LAST, LAST]
        result, *last = second_product(
            me, blocks, starts[c], dense, shared_gate[0], shared_up[0], router_weight[0], pieces
        )
        if c + 1 < chunks:
            partials[0], result = in_order(partials[0], result)
            partials[0] = at("act", c + 1, partials[0])
            own = activation(gate_pre[0], up_pre[0], starts[c + 1], partials)
        result = at("out", c, result)
        sent.append(back_one(result))
    out = jnp.zeros((n, rows, width), jnp.bfloat16)
    for c in range(chunks - 1):
        out = lax.dynamic_update_slice(out, sent[c], (0, starts[c], 0))
    out = put_rows(out, sent[-1], starts[-1])
    length = lax.axis_size("pipe")
    for piece in last:
        near = lax.ppermute(piece, "pipe", [(i, i - 1) for i in range(1, length)])
        far = lax.ppermute(piece, "pipe", [(0, length - 1)])
        out = put_rows(out, near, rows - LAST, "others")
        out = put_rows(out, far, rows - LAST, "last")
    return out.reshape(1, tokens, width)


def solution(mesh):
    in_specs = (
        P("pipe", None, "expert"),
        P("pipe", None, "expert"),
        P("pipe", "expert", None),
        P("pipe", "expert", None),
        P("pipe", "expert", None),
        P("pipe", "expert", None),
        P("pipe", "expert", None),
        P("pipe", None, None),
        P("pipe", None, None),
        P("pipe", None, None),
    )
    out_specs = P("pipe", None, "expert")
    return jax.shard_map(shards, mesh=mesh, in_specs=in_specs, out_specs=out_specs, check_vma=False)
```

```python
import functools

import jax
import jax.numpy as jnp
from jax import lax
from jax.experimental import pallas as pl
from jax.experimental.pallas import tpu as pltpu
from jax.sharding import PartitionSpec as P

PARTS = (3, 5, 4, 4)
LAST = 16
IN_FLIGHT = 2
NEED = {("act", 1): (2,), ("act", 2): (3,)}
WAIT = {("act", 3): (0,), ("mm2", 3): (1,), ("out", 2): (0,), ("out", 3): (1,)}
FREE = pl.CostEstimate(flops=0, bytes_accessed=0, transcendentals=0)


def params(**kwargs):
    return pltpu.CompilerParams(vmem_limit_bytes=48 * 1024 * 1024, **kwargs)


def cut(rows):
    if rows % 256 == 0:
        return [rows // 16 * share for share in PARTS]
    return [rows // 4] * 4 if rows % 64 == 0 else [rows]


def block_of(size, most):
    fits = [b for b in range(128, min(size, most) + 1, 128) if size % b == 0]
    return fits[-1] if fits else size


def back_one(x):
    length = lax.axis_size("pipe")
    return lax.ppermute(x, "pipe", [(i, (i - 1) % length) for i in range(length)])


def to_expert(x, by):
    n = lax.axis_size("expert")
    return lax.ppermute(x, "expert", [(i, (i + by) % n) for i in range(n)])


def to_other_core(x):
    n = lax.axis_size("expert")
    return lax.ppermute(x, "expert", [(i, i ^ 1) for i in range(n)])


def in_hbm(x):
    return pltpu.with_memory_space_constraint(x, pltpu.HBM)


def in_order(later, earlier):
    return lax.optimization_barrier((later, earlier))


def contract_last(left, right):
    return lax.dot_general(
        left, right, (((1,), (1,)), ((), ())), preferred_element_type=jnp.float32
    )


def take_kernel(start, source, target, sems):
    here = pl.ds(start, target.shape[1])
    half = target.shape[0] // 2
    copies = [
        pltpu.make_async_copy(
            source.at[pl.ds(i * half, half), here], target.at[pl.ds(i * half, half)], sems.at[i]
        )
        for i in range(2)
    ]
    for copy in copies:
        copy.start()
    for copy in copies:
        copy.wait()


def put_kernel(start, on, source, old, target, sem):
    del old

    def put():
        here = pl.ds(start, source.shape[1])
        copy = pltpu.make_async_copy(source, target.at[:, here], sem)
        copy.start()
        copy.wait()

    is_last = lax.axis_index("pipe") == lax.axis_size("pipe") - 1
    if on == "all":
        put()
    else:
        pl.when(is_last if on == "last" else jnp.logical_not(is_last))(put)


def take_rows(array, start, size):
    n, _, width = array.shape
    return pl.pallas_call(
        functools.partial(take_kernel, start),
        out_shape=pltpu.VMEM((n, size, width), array.dtype),
        in_specs=[pl.BlockSpec(memory_space=pltpu.HBM)],
        out_specs=pl.BlockSpec(memory_space=pltpu.VMEM),
        scratch_shapes=[pltpu.SemaphoreType.DMA((2,))],
        cost_estimate=FREE,
        name="take_rows",
    )(in_hbm(array))


def put_rows(out, piece, start, on="all"):
    return pl.pallas_call(
        functools.partial(put_kernel, start, on),
        out_shape=jax.ShapeDtypeStruct(out.shape, out.dtype),
        in_specs=[pl.BlockSpec(memory_space=pltpu.VMEM), pl.BlockSpec(memory_space=pltpu.HBM)],
        out_specs=pl.BlockSpec(memory_space=pltpu.HBM),
        scratch_shapes=[pltpu.SemaphoreType.DMA],
        input_output_aliases={1: 0},
        cost_estimate=FREE,
        name="put_rows",
    )(pltpu.with_memory_space_constraint(piece, pltpu.VMEM), out)


def routed_kernel(grad_ref, score_ref, chosen_ref, out_ref):
    grad, scores, chosen = grad_ref[...], score_ref[...], chosen_ref[...]
    total = jnp.sum(scores, axis=0, keepdims=True)
    mixed = jnp.sum(grad * scores, axis=0, keepdims=True)
    logit_grad = 2.5 * (grad - mixed / total) / total * scores * (1.0 - scores)
    experts = lax.broadcasted_iota(jnp.int32, out_ref.shape[::-1], 0)
    dense = jnp.zeros(experts.shape, jnp.float32)
    for slot in range(grad.shape[0]):
        here = chosen[slot : slot + 1] == experts
        dense = dense + jnp.where(here, logit_grad[slot : slot + 1], 0.0)
    out_ref[...] = dense.T.astype(out_ref.dtype)


def routed_grad(grad, scores, chosen, n_experts):
    tokens, top = grad.shape
    block = block_of(tokens, 512)
    spec = pl.BlockSpec((top, block), lambda i: (0, i))
    return pl.pallas_call(
        routed_kernel,
        out_shape=jax.ShapeDtypeStruct((tokens, n_experts), jnp.bfloat16),
        grid=(tokens // block,),
        in_specs=[spec, spec, spec],
        out_specs=pl.BlockSpec((block, n_experts), lambda i: (i, 0)),
        cost_estimate=FREE,
        name="routed_grad",
    )(in_hbm(grad.T), in_hbm(scores.T), in_hbm(chosen.T))


def first_kernel(n, me_ref, rows_ref, weight_ref, *out_refs):
    me = me_ref[0]
    part = rows_ref.shape[1]
    left = jnp.concatenate([rows_ref[lax.rem(me + j, n)] for j in range(n)], axis=0)
    product = contract_last(left, weight_ref[...]).astype(jnp.bfloat16)
    for j in range(n):
        out_refs[j][...] = product[j * part : (j + 1) * part]


def first_product(me, rows, weight, late):
    n, part, width = rows.shape
    hidden = weight.shape[0]
    block = block_of(hidden, 256)
    return pl.pallas_call(
        functools.partial(first_kernel, n),
        out_shape=[jax.ShapeDtypeStruct((part, hidden), jnp.bfloat16)] * n,
        grid_spec=pltpu.PrefetchScalarGridSpec(
            num_scalar_prefetch=1,
            grid=(hidden // block,),
            in_specs=[
                pl.BlockSpec((n, part, width), lambda i, me: (0, 0, 0)),
                pl.BlockSpec((block, width), lambda i, me: (i, 0)),
            ],
            out_specs=[pl.BlockSpec((part, block), lambda i, me: (0, i))] * n,
        ),
        compiler_params=params(),
        cost_estimate=FREE,
        name="first_product",
    )(me, rows, weight if late else in_hbm(weight))


def activation_kernel(start, gate_ref, up_ref, *refs):
    *part_refs, out_ref = refs
    part, hidden = part_refs[0].shape
    here = slice(start, start + part)
    hidden_grad = part_refs[0][...].astype(jnp.float32)
    for ref in part_refs[1:]:
        hidden_grad = hidden_grad + ref[...].astype(jnp.float32)
    act_a = gate_ref[here].astype(jnp.float32)
    act_b = up_ref[here].astype(jnp.float32)
    sigma = 1.0 / (1.0 + jnp.exp(-act_a))
    gate_part = hidden_grad * act_b * sigma * (1.0 + act_a * (1.0 - sigma))
    up_part = hidden_grad * act_a * sigma
    out_ref[:, :hidden] = gate_part.astype(out_ref.dtype)
    out_ref[:, hidden:] = up_part.astype(out_ref.dtype)


def activation(gate_pre, up_pre, start, partials):
    part, hidden = partials[0].shape
    saved = pl.BlockSpec(gate_pre.shape, lambda i: (0, 0))
    return pl.pallas_call(
        functools.partial(activation_kernel, start),
        out_shape=jax.ShapeDtypeStruct((part, 2 * hidden), jnp.bfloat16),
        grid=(1,),
        in_specs=[saved, saved] + [pl.BlockSpec((part, hidden), lambda i: (0, 0))] * len(partials),
        out_specs=pl.BlockSpec((part, 2 * hidden), lambda i: (0, 0)),
        compiler_params=params(),
        cost_estimate=FREE,
        name="activation",
    )(in_hbm(gate_pre), in_hbm(up_pre), *partials)


def second_kernel(n, start, me_ref, dense_ref, gate_ref, up_ref, router_ref, *refs):
    block_refs, out_refs, held = refs[:n], refs[n:-1], refs[-1]
    chips = n // 2
    hidden = gate_ref.shape[1]

    @pl.when(pl.program_id(0) == 0)
    def _():
        me = me_ref[0]
        chip, core = me // 2, lax.rem(me, 2)
        for step in range(chips):
            there = lax.rem(chip - step + chips, chips) * 2
            held[there + core] = block_refs[2 * step][...]
            held[there + 1 - core] = block_refs[2 * step + 1][...]

    both = held[...].reshape(-1, 2 * hidden)
    result = contract_last(both[:, :hidden], gate_ref[...])
    result = result + contract_last(both[:, hidden:], up_ref[...])
    dense = dense_ref[:, start : start + held.shape[1]].reshape(both.shape[0], -1)
    result = result + contract_last(dense, router_ref[...])
    result = result.astype(jnp.bfloat16).reshape(n, held.shape[1], -1)
    first = 0
    for out_ref in out_refs:
        size = out_ref.shape[1]
        out_ref[...] = result[:, first : first + size]
        first += size


def second_product(me, blocks, start, dense, w_gate, w_up, w_router, sizes):
    n = len(blocks)
    part, both = blocks[0].shape
    width, hidden = w_gate.shape
    n_experts = w_router.shape[1]
    block = block_of(width, 256)
    return pl.pallas_call(
        functools.partial(second_kernel, n, start),
        out_shape=[jax.ShapeDtypeStruct((n, size, width), jnp.bfloat16) for size in sizes],
        grid_spec=pltpu.PrefetchScalarGridSpec(
            num_scalar_prefetch=1,
            grid=(width // block,),
            in_specs=[
                pl.BlockSpec(dense.shape, lambda i, me: (0, 0, 0)),
                pl.BlockSpec((block, hidden), lambda i, me: (i, 0)),
                pl.BlockSpec((block, hidden), lambda i, me: (i, 0)),
                pl.BlockSpec((block, n_experts), lambda i, me: (i, 0)),
            ]
            + [pl.BlockSpec((part, both), lambda i, me: (0, 0))] * n,
            out_specs=[pl.BlockSpec((n, size, block), lambda i, me: (0, 0, i)) for size in sizes],
            scratch_shapes=[pltpu.VMEM((n, part, both), jnp.bfloat16)],
        ),
        compiler_params=params(),
        cost_estimate=FREE,
        name="second_product",
    )(me, dense, w_gate, w_up, w_router, *blocks)


def shards(
    upstream,
    shared_down,
    shared_gate,
    shared_up,
    router_weight,
    gate_pre,
    up_pre,
    gate_grad,
    gate_scores,
    expert_ids,
):
    n = lax.axis_size("expert")
    chips = n // 2
    me = lax.axis_index("expert").astype(jnp.int32).reshape(1)
    tokens, width = upstream.shape[1:]
    rows = tokens // n
    sizes = cut(rows)
    starts = [sum(sizes[:c]) for c in range(len(sizes))]
    chunks = len(sizes)
    grads = upstream.reshape(n, rows, width)
    arrived, sent = [], []
    dense = routed_grad(gate_grad[0], gate_scores[0], expert_ids[0], router_weight.shape[2])
    for c in range(chunks):
        if c == 0:
            piece = take_rows(grads, 0, sizes[0])
            grads, dense = in_order(grads, dense)
        else:
            piece = grads[:, starts[c] : starts[c] + sizes[c]]
        if c >= IN_FLIGHT:
            piece, arrived[c - IN_FLIGHT] = in_order(piece, arrived[c - IN_FLIGHT])
        arrived.append(back_one(piece))
    dense = dense.reshape(n, rows, -1)

    def at(point, c, x):
        for p in NEED.get((point, c), ()):
            x, arrived[p] = in_order(x, arrived[p])
        for p in WAIT.get((point, c), ()):
            x, sent[p] = in_order(x, sent[p])
        return x

    def partial_sums(c):
        own, *others = first_product(me, arrived[c], shared_down[0], c > 0)
        others[0] = at("rs", c, others[0])
        return [own] + [to_expert(x, j + 1) for j, x in enumerate(others)]

    arrived[0], dense = in_order(arrived[0], dense)
    own = activation(gate_pre[0], up_pre[0], starts[0], partial_sums(0))
    for c in range(chunks):
        own = at("agy", c, own)
        near = [own] + [to_expert(own, 2 * step) for step in range(1, chips)]
        far = [to_other_core(own)]
        if c + 1 < chunks:
            arrived[c + 1], own = in_order(arrived[c + 1], own)
            partials = partial_sums(c + 1)
            partials[0], near[-1] = in_order(partials[0], near[-1])
        near[-1] = at("agc", c, near[-1])
        far += [to_other_core(x) for x in near[1:]]
        far[-1] = at("mm2", c, far[-1])
        blocks = [x for pair in zip(near, far) for x in pair]
        pieces = [sizes[c]]
        if c + 1 == chunks and sizes[c] > LAST:
            pieces = [sizes[c] - LAST, LAST]
        result, *last = second_product(
            me, blocks, starts[c], dense, shared_gate[0], shared_up[0], router_weight[0], pieces
        )
        if c + 1 < chunks:
            partials[0], result = in_order(partials[0], result)
            partials[0] = at("act", c + 1, partials[0])
            own = activation(gate_pre[0], up_pre[0], starts[c + 1], partials)
        result = at("out", c, result)
        sent.append(back_one(result))
    out = jnp.zeros((n, rows, width), jnp.bfloat16)
    for c in range(chunks - 1):
        out = lax.dynamic_update_slice(out, sent[c], (0, starts[c], 0))
    out = put_rows(out, sent[-1], starts[-1])
    length = lax.axis_size("pipe")
    for piece in last:
        near = lax.ppermute(piece, "pipe", [(i, i - 1) for i in range(1, length)])
        far = lax.ppermute(piece, "pipe", [(0, length - 1)])
        out = put_rows(out, near, rows - LAST, "others")
        out = put_rows(out, far, rows - LAST, "last")
    return out.reshape(1, tokens, width)


def solution(mesh):
    in_specs = (
        P("pipe", None, "expert"),
        P("pipe", None, "expert"),
        P("pipe", "expert", None),
        P("pipe", "expert", None),
        P("pipe", "expert", None),
        P("pipe", "expert", None),
        P("pipe", "expert", None),
        P("pipe", None, None),
        P("pipe", None, None),
        P("pipe", None, None),
    )
    out_specs = P("pipe", None, "expert")
    return jax.shard_map(shards, mesh=mesh, in_specs=in_specs, out_specs=out_specs, check_vma=False)
```

```python
import functools

import jax
import jax.numpy as jnp
from jax import lax
from jax.experimental import pallas as pl
from jax.experimental.pallas import tpu as pltpu
from jax.sharding import PartitionSpec as P

PARTS = (3, 5, 4, 4)
LAST = 16
IN_FLIGHT = 2
NEED = {("act", 1): (2,), ("act", 2): (3,)}
WAIT = {("act", 3): (0,), ("mm2", 3): (1,), ("out", 2): (0,), ("out", 3): (1,)}
FREE = pl.CostEstimate(flops=0, bytes_accessed=0, transcendentals=0)


def params(**kwargs):
    return pltpu.CompilerParams(vmem_limit_bytes=48 * 1024 * 1024, **kwargs)


def cut(rows):
    if rows % 256 == 0:
        return [rows // 16 * share for share in PARTS]
    return [rows // 4] * 4 if rows % 64 == 0 else [rows]


def block_of(size, most):
    fits = [b for b in range(128, min(size, most) + 1, 128) if size % b == 0]
    return fits[-1] if fits else size


def back_one(x):
    length = lax.axis_size("pipe")
    return lax.ppermute(x, "pipe", [(i, (i - 1) % length) for i in range(length)])


def to_expert(x, by):
    n = lax.axis_size("expert")
    return lax.ppermute(x, "expert", [(i, (i + by) % n) for i in range(n)])


def to_other_core(x):
    n = lax.axis_size("expert")
    return lax.ppermute(x, "expert", [(i, i ^ 1) for i in range(n)])


def in_hbm(x):
    return pltpu.with_memory_space_constraint(x, pltpu.HBM)


def in_order(later, earlier):
    return lax.optimization_barrier((later, earlier))


def contract_last(left, right):
    return lax.dot_general(
        left, right, (((1,), (1,)), ((), ())), preferred_element_type=jnp.float32
    )


def take_kernel(start, source, target, sems):
    here = pl.ds(start, target.shape[1])
    half = target.shape[0] // 2
    copies = [
        pltpu.make_async_copy(
            source.at[pl.ds(i * half, half), here], target.at[pl.ds(i * half, half)], sems.at[i]
        )
        for i in range(2)
    ]
    for copy in copies:
        copy.start()
    for copy in copies:
        copy.wait()


def put_kernel(start, on, source, old, target, sem):
    del old

    def put():
        here = pl.ds(start, source.shape[1])
        copy = pltpu.make_async_copy(source, target.at[:, here], sem)
        copy.start()
        copy.wait()

    is_last = lax.axis_index("pipe") == lax.axis_size("pipe") - 1
    if on == "all":
        put()
    else:
        pl.when(is_last if on == "last" else jnp.logical_not(is_last))(put)


def take_rows(array, start, size):
    n, _, width = array.shape
    return pl.pallas_call(
        functools.partial(take_kernel, start),
        out_shape=pltpu.VMEM((n, size, width), array.dtype),
        in_specs=[pl.BlockSpec(memory_space=pltpu.HBM)],
        out_specs=pl.BlockSpec(memory_space=pltpu.VMEM),
        scratch_shapes=[pltpu.SemaphoreType.DMA((2,))],
        cost_estimate=FREE,
        name="take_rows",
    )(in_hbm(array))


def put_rows(out, piece, start, on="all"):
    return pl.pallas_call(
        functools.partial(put_kernel, start, on),
        out_shape=jax.ShapeDtypeStruct(out.shape, out.dtype),
        in_specs=[pl.BlockSpec(memory_space=pltpu.VMEM), pl.BlockSpec(memory_space=pltpu.HBM)],
        out_specs=pl.BlockSpec(memory_space=pltpu.HBM),
        scratch_shapes=[pltpu.SemaphoreType.DMA],
        input_output_aliases={1: 0},
        cost_estimate=FREE,
        name="put_rows",
    )(pltpu.with_memory_space_constraint(piece, pltpu.VMEM), out)


def routed_kernel(grad_ref, score_ref, chosen_ref, out_ref):
    grad, scores, chosen = grad_ref[...], score_ref[...], chosen_ref[...]
    total = jnp.sum(scores, axis=0, keepdims=True)
    mixed = jnp.sum(grad * scores, axis=0, keepdims=True)
    logit_grad = 2.5 * (grad - mixed / total) / total * scores * (1.0 - scores)
    experts = lax.broadcasted_iota(jnp.int32, out_ref.shape[::-1], 0)
    dense = jnp.zeros(experts.shape, jnp.float32)
    for slot in range(grad.shape[0]):
        here = chosen[slot : slot + 1] == experts
        dense = dense + jnp.where(here, logit_grad[slot : slot + 1], 0.0)
    out_ref[...] = dense.T.astype(out_ref.dtype)


def routed_grad(grad, scores, chosen, n_experts):
    tokens, top = grad.shape
    block = block_of(tokens, 1024)
    spec = pl.BlockSpec((top, block), lambda i: (0, i))
    return pl.pallas_call(
        routed_kernel,
        out_shape=jax.ShapeDtypeStruct((tokens, n_experts), jnp.bfloat16),
        grid=(tokens // block,),
        in_specs=[spec, spec, spec],
        out_specs=pl.BlockSpec((block, n_experts), lambda i: (i, 0)),
        cost_estimate=FREE,
        name="routed_grad",
    )(in_hbm(grad.T), in_hbm(scores.T), in_hbm(chosen.T))


def first_kernel(n, me_ref, rows_ref, weight_ref, *out_refs):
    me = me_ref[0]
    part = rows_ref.shape[1]
    left = jnp.concatenate([rows_ref[lax.rem(me + j, n)] for j in range(n)], axis=0)
    product = contract_last(left, weight_ref[...]).astype(jnp.bfloat16)
    for j in range(n):
        out_refs[j][...] = product[j * part : (j + 1) * part]


def first_product(me, rows, weight, late):
    n, part, width = rows.shape
    hidden = weight.shape[0]
    block = block_of(hidden, 256)
    return pl.pallas_call(
        functools.partial(first_kernel, n),
        out_shape=[jax.ShapeDtypeStruct((part, hidden), jnp.bfloat16)] * n,
        grid_spec=pltpu.PrefetchScalarGridSpec(
            num_scalar_prefetch=1,
            grid=(hidden // block,),
            in_specs=[
                pl.BlockSpec((n, part, width), lambda i, me: (0, 0, 0)),
                pl.BlockSpec((block, width), lambda i, me: (i, 0)),
            ],
            out_specs=[pl.BlockSpec((part, block), lambda i, me: (0, i))] * n,
        ),
        compiler_params=params(),
        cost_estimate=FREE,
        name="first_product",
    )(me, rows, weight if late else in_hbm(weight))


def activation_kernel(start, gate_ref, up_ref, *refs):
    *part_refs, out_ref = refs
    part, hidden = part_refs[0].shape
    here = slice(start, start + part)
    hidden_grad = part_refs[0][...].astype(jnp.float32)
    for ref in part_refs[1:]:
        hidden_grad = hidden_grad + ref[...].astype(jnp.float32)
    act_a = gate_ref[here].astype(jnp.float32)
    act_b = up_ref[here].astype(jnp.float32)
    sigma = 1.0 / (1.0 + jnp.exp(-act_a))
    gate_part = hidden_grad * act_b * sigma * (1.0 + act_a * (1.0 - sigma))
    up_part = hidden_grad * act_a * sigma
    out_ref[:, :hidden] = gate_part.astype(out_ref.dtype)
    out_ref[:, hidden:] = up_part.astype(out_ref.dtype)


def activation(gate_pre, up_pre, start, partials):
    part, hidden = partials[0].shape
    saved = pl.BlockSpec(gate_pre.shape, lambda i: (0, 0))
    return pl.pallas_call(
        functools.partial(activation_kernel, start),
        out_shape=jax.ShapeDtypeStruct((part, 2 * hidden), jnp.bfloat16),
        grid=(1,),
        in_specs=[saved, saved] + [pl.BlockSpec((part, hidden), lambda i: (0, 0))] * len(partials),
        out_specs=pl.BlockSpec((part, 2 * hidden), lambda i: (0, 0)),
        compiler_params=params(),
        cost_estimate=FREE,
        name="activation",
    )(in_hbm(gate_pre), in_hbm(up_pre), *partials)


def second_kernel(n, start, me_ref, dense_ref, gate_ref, up_ref, router_ref, *refs):
    block_refs, out_refs, held = refs[:n], refs[n:-1], refs[-1]
    chips = n // 2
    hidden = gate_ref.shape[1]

    @pl.when(pl.program_id(0) == 0)
    def _():
        me = me_ref[0]
        chip, core = me // 2, lax.rem(me, 2)
        for step in range(chips):
            there = lax.rem(chip - step + chips, chips) * 2
            held[there + core] = block_refs[2 * step][...]
            held[there + 1 - core] = block_refs[2 * step + 1][...]

    both = held[...].reshape(-1, 2 * hidden)
    result = contract_last(both[:, :hidden], gate_ref[...])
    result = result + contract_last(both[:, hidden:], up_ref[...])
    dense = dense_ref[:, start : start + held.shape[1]].reshape(both.shape[0], -1)
    result = result + contract_last(dense, router_ref[...])
    result = result.astype(jnp.bfloat16).reshape(n, held.shape[1], -1)
    first = 0
    for out_ref in out_refs:
        size = out_ref.shape[1]
        out_ref[...] = result[:, first : first + size]
        first += size


def second_product(me, blocks, start, dense, w_gate, w_up, w_router, sizes):
    n = len(blocks)
    part, both = blocks[0].shape
    width, hidden = w_gate.shape
    n_experts = w_router.shape[1]
    block = block_of(width, 256)
    return pl.pallas_call(
        functools.partial(second_kernel, n, start),
        out_shape=[jax.ShapeDtypeStruct((n, size, width), jnp.bfloat16) for size in sizes],
        grid_spec=pltpu.PrefetchScalarGridSpec(
            num_scalar_prefetch=1,
            grid=(width // block,),
            in_specs=[
                pl.BlockSpec(dense.shape, lambda i, me: (0, 0, 0)),
                pl.BlockSpec((block, hidden), lambda i, me: (i, 0)),
                pl.BlockSpec((block, hidden), lambda i, me: (i, 0)),
                pl.BlockSpec((block, n_experts), lambda i, me: (i, 0)),
            ]
            + [pl.BlockSpec((part, both), lambda i, me: (0, 0))] * n,
            out_specs=[pl.BlockSpec((n, size, block), lambda i, me: (0, 0, i)) for size in sizes],
            scratch_shapes=[pltpu.VMEM((n, part, both), jnp.bfloat16)],
        ),
        compiler_params=params(),
        cost_estimate=FREE,
        name="second_product",
    )(me, dense, w_gate, w_up, w_router, *blocks)


def shards(
    upstream,
    shared_down,
    shared_gate,
    shared_up,
    router_weight,
    gate_pre,
    up_pre,
    gate_grad,
    gate_scores,
    expert_ids,
):
    n = lax.axis_size("expert")
    chips = n // 2
    me = lax.axis_index("expert").astype(jnp.int32).reshape(1)
    tokens, width = upstream.shape[1:]
    rows = tokens // n
    sizes = cut(rows)
    starts = [sum(sizes[:c]) for c in range(len(sizes))]
    chunks = len(sizes)
    grads = upstream.reshape(n, rows, width)
    arrived, sent = [], []
    dense = routed_grad(gate_grad[0], gate_scores[0], expert_ids[0], router_weight.shape[2])
    for c in range(chunks):
        if c == 0:
            piece = take_rows(grads, 0, sizes[0])
            grads, dense = in_order(grads, dense)
        else:
            piece = grads[:, starts[c] : starts[c] + sizes[c]]
        if c >= IN_FLIGHT:
            piece, arrived[c - IN_FLIGHT] = in_order(piece, arrived[c - IN_FLIGHT])
        arrived.append(back_one(piece))
    dense = dense.reshape(n, rows, -1)

    def at(point, c, x):
        for p in NEED.get((point, c), ()):
            x, arrived[p] = in_order(x, arrived[p])
        for p in WAIT.get((point, c), ()):
            x, sent[p] = in_order(x, sent[p])
        return x

    def partial_sums(c):
        own, *others = first_product(me, arrived[c], shared_down[0], c > 0)
        others[0] = at("rs", c, others[0])
        return [own] + [to_expert(x, j + 1) for j, x in enumerate(others)]

    arrived[0], dense = in_order(arrived[0], dense)
    own = activation(gate_pre[0], up_pre[0], starts[0], partial_sums(0))
    for c in range(chunks):
        own = at("agy", c, own)
        near = [own] + [to_expert(own, 2 * step) for step in range(1, chips)]
        far = [to_other_core(own)]
        if c + 1 < chunks:
            arrived[c + 1], own = in_order(arrived[c + 1], own)
            partials = partial_sums(c + 1)
            partials[0], near[-1] = in_order(partials[0], near[-1])
        near[-1] = at("agc", c, near[-1])
        far += [to_other_core(x) for x in near[1:]]
        far[-1] = at("mm2", c, far[-1])
        blocks = [x for pair in zip(near, far) for x in pair]
        pieces = [sizes[c]]
        if c + 1 == chunks and sizes[c] > LAST:
            pieces = [sizes[c] - LAST, LAST]
        result, *last = second_product(
            me, blocks, starts[c], dense, shared_gate[0], shared_up[0], router_weight[0], pieces
        )
        if c + 1 < chunks:
            partials[0], result = in_order(partials[0], result)
            partials[0] = at("act", c + 1, partials[0])
            own = activation(gate_pre[0], up_pre[0], starts[c + 1], partials)
        result = at("out", c, result)
        sent.append(back_one(result))
    out = jnp.zeros((n, rows, width), jnp.bfloat16)
    for c in range(chunks - 1):
        out = lax.dynamic_update_slice(out, sent[c], (0, starts[c], 0))
    out = put_rows(out, sent[-1], starts[-1])
    length = lax.axis_size("pipe")
    for piece in last:
        near = lax.ppermute(piece, "pipe", [(i, i - 1) for i in range(1, length)])
        far = lax.ppermute(piece, "pipe", [(0, length - 1)])
        out = put_rows(out, near, rows - LAST, "others")
        out = put_rows(out, far, rows - LAST, "last")
    return out.reshape(1, tokens, width)


def solution(mesh):
    in_specs = (
        P("pipe", None, "expert"),
        P("pipe", None, "expert"),
        P("pipe", "expert", None),
        P("pipe", "expert", None),
        P("pipe", "expert", None),
        P("pipe", "expert", None),
        P("pipe", "expert", None),
        P("pipe", None, None),
        P("pipe", None, None),
        P("pipe", None, None),
    )
    out_specs = P("pipe", None, "expert")
    return jax.shard_map(shards, mesh=mesh, in_specs=in_specs, out_specs=out_specs, check_vma=False)
```
